128 devices in a mesh: section: 2 (over x_hi), seq: 8 (over y, core), rep: 8 (over x_lo, z).
Axes of the slice: x: 4 (x_hi: 2, x_lo: 2; x = x_hi * 2 + x_lo), y: 4, z: 4, core: 2. Of those that a mesh axis runs over, the one named last changes fastest.
Arguments:
- tokens_in: bfloat16 [8, 4096, 1024], P('rep', 'seq')
- lengths: int32 [8], P('rep'), may hold values from 1024 to 4096, as said below
- cotangent: bfloat16 [8, 4096, 1024], P('rep', 'seq')
- time_blocks: bfloat16 [2, 64, 64, 64], P('section', 'seq'), may hold values from -0.75 to 0.75
- spectral_blocks: bfloat16 [2, 64, 64, 64], P('section', 'seq'), may hold values from -0.75 to 0.75
- spectral_kernel: bfloat16 [2, 64, 64, 1024], P('section', 'seq'), may hold values from -6 to 6
- gate_weight: bfloat16 [2, 4, 256, 1024], P('section'), may hold values from -0.375 to 0.375
- up_weight: bfloat16 [2, 4, 256, 1024], P('section'), may hold values from -0.375 to 0.375
- down_weight: bfloat16 [2, 4, 1024, 256], P('section'), may hold values from -0.1875 to 0.1875
- momentum_time: float32 [2, 64, 64, 64], P('section', 'seq', 'rep'), may hold values from -6 to 6
- momentum_spectral: float32 [2, 64, 64, 64], P('section', 'seq', 'rep'), may hold values from -6 to 6
- momentum_kernel: float32 [2, 64, 64, 1024], P('section', 'seq', None, 'rep'), may hold values from -6 to 6
- momentum_gate: float32 [2, 4, 256, 1024], P('section', None, None, ('seq', 'rep')), may hold values from -6 to 6
- momentum_up: float32 [2, 4, 256, 1024], P('section', None, None, ('seq', 'rep')), may hold values from -6 to 6
- momentum_down: float32 [2, 4, 1024, 256], P('section', None, ('seq', 'rep')), may hold values from -6 to 6
Outputs:
- new_time: float32 [2, 64, 64, 64], P('section', 'seq', 'rep')
- new_spectral: float32 [2, 64, 64, 64], P('section', 'seq', 'rep')
- new_kernel: float32 [2, 64, 64, 1024], P('section', 'seq', None, 'rep')
- new_gate: float32 [2, 4, 256, 1024], P('section', None, None, ('seq', 'rep'))
- new_up: float32 [2, 4, 256, 1024], P('section', None, None, ('seq', 'rep'))
- new_down: float32 [2, 4, 1024, 256], P('section', None, ('seq', 'rep'))
The draws below stay inside these ranges and needn't reach their ends.
Inputs may be any that keep to these rules, and one draw needn't show every extreme that they name: `lengths`: the first sequence has all 4096 positions live and the second a quarter of them.
All inputs are finite; a program needn't handle non-finite values.
Results may differ from the reference program's by a relative error of at most 0.02.
Values may be sent and summed in bfloat16 or wider, within the bound.
No kernel may reach another device: no remote copies, remote signals or barrier semaphores. Data moves between devices by JAX's collectives and lax.ppermute only.
A program may use at most 192 MiB of HBM per device.

```python
import jax
import jax.numpy as jnp
from jax import lax

D = 1024
FF = 4096
NB = 4
S1 = 64
S2 = 64
SEQS = 1
N_SECTION = 2
N_REP = 8


def draw_lengths(key, part):
    key = jax.random.fold_in(key, 11)
    full_length = S1 * S2
    drawn = jax.random.randint(key, (N_REP * SEQS,), full_length // 4, full_length + 1)
    drawn = drawn.at[0].set(full_length)
    drawn = drawn.at[1].set(full_length // 4)
    return drawn.astype(jnp.int32)


def draw_tokens_in(key, part):
    key = jax.random.fold_in(key, 37)
    common_key, own_key = jax.random.split(key)
    full_length = S1 * S2
    common = jnp.clip(jax.random.normal(common_key, (full_length, D), jnp.float32), -4.0, 4.0)
    own = jnp.clip(jax.random.normal(own_key, (N_REP * SEQS, full_length, D), jnp.float32), -4.0, 4.0)
    values = 0.6 * common[None, :, :] + 0.8 * own
    return values.astype(jnp.bfloat16)


def draw_cotangent(key, part):
    key = jax.random.fold_in(key, 23)
    first_key = jax.random.fold_in(key, 0)
    common_key = jax.random.fold_in(key, 2)
    full_length = S1 * S2
    position_ramp = 0.5 + jnp.arange(full_length, dtype=jnp.float32) / full_length
    common = jnp.clip(jax.random.normal(common_key, (full_length, D), jnp.float32), -4.0, 4.0)
    base_draw = jnp.clip(jax.random.normal(first_key, (N_REP * SEQS, full_length, D), jnp.float32), -4.0, 4.0)
    values = (0.6 * common[None, :, :] + 0.8 * base_draw) * position_ramp[None, :, None]
    return values.astype(jnp.bfloat16)


def levels(key, shape, pieces, low, largest):
    def one(axis_at, blocks):
        draws = jax.random.uniform(jax.random.fold_in(jax.random.fold_in(key, 6), axis_at), (blocks,), jnp.float32, low / len(pieces), largest / len(pieces))
        return jnp.repeat(jnp.exp(draws), shape[axis_at] // blocks).reshape((-1,) + (1,) * (len(shape) - axis_at - 1))

    loudness = one(*pieces[0])
    for cut in pieces[1:]:
        loudness = loudness * one(*cut)
    return loudness


def scatter_about(rng, shape, scale, limit, cuts=(), kind=jnp.bfloat16):
    entries = jax.random.normal(rng, shape, jnp.float32) * scale
    if len(cuts) > 0:
        entries = levels(rng, shape, cuts, -0.22, 0.18) * entries
    return jnp.clip(entries, min=-limit, max=limit).astype(kind)


def setup_inputs(seed: int = 0) -> dict:
    streams_of = jax.random.split(jax.random.key(seed), 16)
    tokens_in = draw_tokens_in(jax.random.fold_in(streams_of[15], 71), 0)
    lengths = draw_lengths(jax.random.fold_in(streams_of[15], 71), 0)
    cotangent = draw_cotangent(jax.random.fold_in(streams_of[15], 71), 0)
    time_blocks = scatter_about(streams_of[3], (N_SECTION, S1, S2, S2), S2 ** -0.5, 0.75, ((0, 2), (1, 8)))
    spectral_blocks = scatter_about(streams_of[4], (N_SECTION, S2, S1, S1), S1 ** -0.5, 0.75, ((0, 2), (1, 8)))
    spectral_kernel = scatter_about(streams_of[5], (N_SECTION, S2, S1, D), 1.0, 6.0, ((0, 2), (1, 8)))
    gate_weight = scatter_about(streams_of[6], (N_SECTION, NB, D // NB, FF // NB), (D // NB) ** -0.5, 0.375, ((0, 2),))
    up_weight = scatter_about(streams_of[7], (N_SECTION, NB, D // NB, FF // NB), (D // NB) ** -0.5, 0.375, ((0, 2),))
    down_weight = scatter_about(streams_of[8], (N_SECTION, NB, FF // NB, D // NB), (FF // NB) ** -0.5, 0.1875, ((0, 2),))
    momentum_time = scatter_about(streams_of[9], (N_SECTION, S1, S2, S2), 1.0, 6.0, ((0, 2), (1, 8), (2, 8)), jnp.float32)
    momentum_spectral = scatter_about(streams_of[10], (N_SECTION, S2, S1, S1), 1.0, 6.0, ((0, 2), (1, 8), (2, 8)), jnp.float32)
    momentum_kernel = scatter_about(streams_of[11], (N_SECTION, S2, S1, D), 1.0, 6.0, ((0, 2), (1, 8), (3, 8)), jnp.float32)
    momentum_gate = scatter_about(streams_of[12], (N_SECTION, NB, D // NB, FF // NB), 1.0, 6.0, ((0, 2), (3, 64)), jnp.float32)
    momentum_up = scatter_about(streams_of[13], (N_SECTION, NB, D // NB, FF // NB), 1.0, 6.0, ((0, 2), (3, 64)), jnp.float32)
    momentum_down = scatter_about(streams_of[14], (N_SECTION, NB, FF // NB, D // NB), 1.0, 6.0, ((0, 2), (2, 64)), jnp.float32)
    return dict(tokens_in=tokens_in, lengths=lengths, cotangent=cotangent, time_blocks=time_blocks, spectral_blocks=spectral_blocks, spectral_kernel=spectral_kernel, gate_weight=gate_weight, up_weight=up_weight, down_weight=down_weight, momentum_time=momentum_time, momentum_spectral=momentum_spectral, momentum_kernel=momentum_kernel, momentum_gate=momentum_gate, momentum_up=momentum_up, momentum_down=momentum_down)


momentum_coef = 0.9
norm_eps = 1e-06

def batched(pattern, first_operand, second_operand):
    return jnp.einsum(pattern, first_operand.astype(jnp.float32), second_operand.astype(jnp.float32))

def mixer_forward(time_mix, spectral_mix, kernel, inputs):
    width = inputs.shape[1]
    time_major = inputs.reshape(S1, S2, width)
    first_mix = batched('aij,ajc->aic', time_mix, time_major).astype(jnp.bfloat16)
    columns = jnp.transpose(first_mix, (1, 0, 2))
    spectrum = batched('bij,bjc->bic', spectral_mix, columns)
    weighted = (kernel.astype(jnp.float32) * spectrum).astype(jnp.bfloat16)
    returned = batched('bji,bjc->bic', spectral_mix, weighted).astype(jnp.bfloat16)
    rows_back = jnp.transpose(returned, (1, 0, 2))
    mixed = batched('aji,ajc->aic', time_mix, rows_back)
    hidden = (inputs.astype(jnp.float32) + mixed.reshape(S1 * S2, width)).astype(jnp.bfloat16)
    return (hidden, (time_major, columns, spectrum, weighted, rows_back))

def mixer_backward(time_mix, spectral_mix, kernel, stored, grad_hidden):
    time_major, columns, spectrum, weighted, rows_back = stored
    width = grad_hidden.shape[1]
    grad_mixed = grad_hidden.astype(jnp.bfloat16).reshape(S1, S2, width)
    time_grad = batched('aic,ajc->aij', rows_back, grad_mixed)
    grad_back = batched('aij,ajc->aic', time_mix, grad_mixed).astype(jnp.bfloat16)
    grad_cols = jnp.transpose(grad_back, (1, 0, 2))
    grad_weighted = batched('bji,bic->bjc', spectral_mix, grad_cols)
    spectral_grad = batched('bjc,bic->bji', weighted, grad_cols)
    kernel_grad = grad_weighted * spectrum
    grad_spectrum = (grad_weighted * kernel.astype(jnp.float32)).astype(jnp.bfloat16)
    grad_columns = batched('bij,bic->bjc', spectral_mix, grad_spectrum).astype(jnp.bfloat16)
    spectral_grad = spectral_grad + batched('bic,bjc->bij', grad_spectrum, columns)
    grad_rows = jnp.transpose(grad_columns, (1, 0, 2))
    grad_inputs = batched('aij,aic->ajc', time_mix, grad_rows)
    time_grad = time_grad + batched('aic,ajc->aij', grad_rows, time_major)
    grad_entry = (grad_hidden + grad_inputs.reshape(S1 * S2, width)).astype(jnp.bfloat16)
    return (grad_entry, (time_grad, spectral_grad, kernel_grad))

def block_mlp(gate_weight, up_weight, down_weight, hidden):
    blocks = gate_weight.shape[0]
    row_count, width = hidden.shape
    wide = hidden.astype(jnp.float32)
    inv_rms = lax.rsqrt(lax.optimization_barrier(jnp.mean(wide * wide, axis=-1, keepdims=True)) + norm_eps)
    normed = (wide * inv_rms).astype(jnp.bfloat16).reshape(row_count, blocks, width // blocks)
    gate = batched('rkd,kdf->rkf', normed, gate_weight)
    upper = batched('rkd,kdf->rkf', normed, up_weight)
    active = (jax.nn.silu(gate) * upper).astype(jnp.bfloat16)
    lowered = batched('rkf,kfd->rkd', active, down_weight).reshape(row_count, width)
    output = (wide + lowered).astype(jnp.bfloat16)
    return (output, (inv_rms, normed, gate, upper, active))

def mlp_backward(gate_weight, up_weight, down_weight, hidden, stored, upstream):
    inv_rms, normed, gate, upper, active = stored
    blocks = gate_weight.shape[0]
    row_count, width = hidden.shape
    cot_blocks = upstream.reshape(row_count, blocks, width // blocks)
    grad_down = batched('rkf,rkd->kfd', active, cot_blocks)
    grad_active = batched('rkd,kfd->rkf', cot_blocks, down_weight)
    sigma = jax.nn.sigmoid(gate)
    grad_gate = (grad_active * upper * sigma * (1.0 + gate * (1.0 - sigma))).astype(jnp.bfloat16)
    grad_upper = (grad_active * gate * sigma).astype(jnp.bfloat16)
    grad_gate_weight = batched('rkd,rkf->kdf', normed, grad_gate)
    grad_up_weight = batched('rkd,rkf->kdf', normed, grad_upper)
    grad_normed = batched('rkf,kdf->rkd', grad_gate, gate_weight) + batched('rkf,kdf->rkd', grad_upper, up_weight)
    grad_normed = grad_normed.reshape(row_count, width)
    wide = hidden.astype(jnp.float32)
    centred = lax.optimization_barrier(jnp.mean(grad_normed * wide, axis=-1, keepdims=True))
    grad_hidden = upstream.astype(jnp.float32) + inv_rms * grad_normed - wide * inv_rms ** 3 * centred
    return (grad_hidden, (grad_gate_weight, grad_up_weight, grad_down))

def reference(tokens_in, lengths, cotangent, time_blocks, spectral_blocks, spectral_kernel, gate_weight, up_weight, down_weight, momentum_time, momentum_spectral, momentum_kernel, momentum_gate, momentum_up, momentum_down):
    section_count = time_blocks.shape[0]
    positions = jnp.arange(S1 * S2, dtype=jnp.int32)
    weights = [(time_blocks[section_number], spectral_blocks[section_number], spectral_kernel[section_number], gate_weight[section_number], up_weight[section_number], down_weight[section_number]) for section_number in range(section_count)]
    totals = [tuple((jnp.zeros(member.shape, jnp.float32) for member in section_weights)) for section_weights in weights]
    for sequence in range(N_REP * SEQS):
        keep_mask = (positions < lengths[sequence])[:, None]
        activations = jnp.where(keep_mask, tokens_in[sequence], jnp.zeros_like(tokens_in[sequence]))
        stored = []
        for section_number in range(section_count):
            section_weights = weights[section_number]
            hidden, mix_saved = mixer_forward(section_weights[0], section_weights[1], section_weights[2], activations)
            activations, mlp_saved = block_mlp(section_weights[3], section_weights[4], section_weights[5], hidden)
            stored.append((hidden, mix_saved, mlp_saved))
        upstream = jnp.where(keep_mask, cotangent[sequence], jnp.zeros_like(cotangent[sequence]))
        for section_number in reversed(range(section_count)):
            section_weights = weights[section_number]
            hidden, mix_saved, mlp_saved = stored[section_number]
            grad_hidden, mlp_grads = mlp_backward(section_weights[3], section_weights[4], section_weights[5], hidden, mlp_saved, upstream)
            upstream, mix_grads = mixer_backward(section_weights[0], section_weights[1], section_weights[2], mix_saved, grad_hidden)
            totals[section_number] = tuple((running + update_term for running, update_term in zip(totals[section_number], mix_grads + mlp_grads)))
    momenta = (momentum_time, momentum_spectral, momentum_kernel, momentum_gate, momentum_up, momentum_down)
    results = []
    for member in range(6):
        stacked = jnp.stack([totals[section_number][member] for section_number in range(section_count)])
        entry_axes = tuple(range(1, stacked.ndim))
        inv_scale = lax.rsqrt(lax.optimization_barrier(jnp.mean(stacked * stacked, axis=entry_axes, keepdims=True)) + norm_eps)
        results.append(momentum_coef * momenta[member] + stacked * inv_scale)
    return (results[0], results[1], results[2], results[3], results[4], results[5])
```

```python
import jax
import jax.numpy as jnp
from jax import lax
from jax.sharding import Mesh
from jax.sharding import PartitionSpec as P

momentum_coef = 0.9
norm_eps = 1e-06
BF = jnp.bfloat16
F32 = jnp.float32


def product(pattern, first_operand, second_operand):
    return jnp.einsum(pattern, first_operand, second_operand, preferred_element_type=F32)


def core_swap(value):
    return lax.ppermute(value, "core", [(0, 1), (1, 0)])


def section_swap(value):
    return lax.ppermute(value, "section", [(0, 1), (1, 0)])


def sum_over_y(value):
    count = lax.axis_size("y")
    total = value
    for step in range(1, count):
        total = total + lax.ppermute(value, "y", [(i, (i + step) % count) for i in range(count)])
    return total


def time_mix_forward(time_mix, values):
    mixed = product("aij,ajc->iac", time_mix, values).astype(BF)
    half = mixed.shape[0] // 2
    return mixed[:half], mixed[half:]


def to_columns(time_mix, values):
    own, other = time_mix_forward(time_mix, values)
    return jnp.concatenate([own, core_swap(other)], axis=1)


def to_rows(blocks):
    half = blocks.shape[1] // 2
    own, other = blocks[:, :half], blocks[:, half:]
    return jnp.concatenate([own, core_swap(other)], axis=0)


def mixer_forward(time_mix, spectral_mix, kernel, inputs):
    columns = to_columns(time_mix, inputs)
    spectrum = product("bij,bjc->bic", spectral_mix, columns)
    weighted = (kernel.astype(F32) * spectrum).astype(BF)
    returned = product("bji,bjc->bic", spectral_mix, weighted).astype(BF)
    rows_back = to_rows(returned)
    mixed = product("aji,jac->aic", time_mix, rows_back)
    hidden = (inputs.astype(F32) + mixed).astype(BF)
    return hidden, (inputs, columns, spectrum, weighted, rows_back)


def mixer_backward(time_mix, spectral_mix, kernel, stored, grad_hidden, need_entry):
    inputs, columns, spectrum, weighted, rows_back = stored
    grad_mixed = grad_hidden.astype(BF)
    grad_cols = to_columns(time_mix, grad_mixed)
    time_grad = product("iac,ajc->aij", rows_back, grad_mixed)
    grad_weighted = product("bji,bic->bjc", spectral_mix, grad_cols)
    spectral_grad = product("bjc,bic->bji", weighted, grad_cols)
    kernel_grad = (grad_weighted * spectrum).astype(BF)
    grad_spectrum = (grad_weighted * kernel.astype(F32)).astype(BF)
    grad_columns = product("bij,bic->bjc", spectral_mix, grad_spectrum).astype(BF)
    spectral_grad = spectral_grad + product("bic,bjc->bij", grad_spectrum, columns)
    grad_rows = to_rows(grad_columns)
    time_grad = time_grad + product("iac,ajc->aij", grad_rows, inputs)
    entry = None
    if need_entry:
        entry = (grad_hidden + product("aij,iac->ajc", time_mix, grad_rows)).astype(BF)
    return entry, (time_grad.astype(BF), spectral_grad.astype(BF), kernel_grad)


def mlp_forward(weights, hidden, width, need_output):
    gate_weight, up_weight, down_weight = weights
    wide = hidden.astype(F32)
    inv_rms = lax.rsqrt(sum_over_y(jnp.sum(wide * wide, axis=-1)) / width + norm_eps)[..., None]
    normed = (wide * inv_rms).astype(BF)
    gate = product("rd,df->rf", normed, gate_weight)
    upper = product("rd,df->rf", normed, up_weight)
    active = (jax.nn.silu(gate) * upper).astype(BF)
    output = None
    if need_output:
        output = (wide + product("rf,fd->rd", active, down_weight)).astype(BF)
    return output, (inv_rms, normed, gate, upper, active)


def mlp_backward(weights, hidden, stored, upstream, width):
    gate_weight, up_weight, down_weight = weights
    inv_rms, normed, gate, upper, active = stored
    grad_down = product("rf,rd->fd", active, upstream)
    grad_active = product("rd,fd->rf", upstream, down_weight)
    sigma = jax.nn.sigmoid(gate)
    grad_gate = (grad_active * upper * sigma * (1.0 + gate * (1.0 - sigma))).astype(BF)
    grad_upper = (grad_active * gate * sigma).astype(BF)
    grad_normed = product("rf,df->rd", grad_gate, gate_weight) + product("rf,df->rd", grad_upper, up_weight)
    wide = hidden.astype(F32)
    centred = sum_over_y(jnp.sum(grad_normed * wide, axis=-1))[..., None] / width
    grad_gate_weight = product("rf,rd->fd", grad_gate, normed)
    grad_up_weight = product("rf,rd->fd", grad_upper, normed)
    grad_hidden = upstream.astype(F32) + inv_rms * grad_normed - wide * inv_rms**3 * centred
    return grad_hidden, jnp.stack([grad_gate_weight, grad_up_weight, grad_down]).astype(BF)


def spread_rows(values):
    ny = lax.axis_size("y")
    rows, width = values.shape
    pieces = jnp.transpose(values.reshape(rows, ny, width // ny), (1, 0, 2))
    return lax.all_to_all(pieces, "y", 0, 0, tiled=True).reshape(ny * rows, width // ny)


def shards(
    tokens_in,
    lengths,
    cotangent,
    time_blocks,
    spectral_blocks,
    spectral_kernel,
    gate_weight,
    up_weight,
    down_weight,
    momentum_time,
    momentum_spectral,
    momentum_kernel,
    momentum_gate,
    momentum_up,
    momentum_down,
):
    ny, nc, nr = lax.axis_size("y"), lax.axis_size("core"), lax.axis_size("rep")
    section, y, core = lax.axis_index("section"), lax.axis_index("y"), lax.axis_index("core")
    _, row_count, width = tokens_in.shape
    block = width // ny
    per = time_blocks.shape[1]
    size = time_blocks.shape[2]
    mine = per * ny
    first_layer = section == 0

    positions = (y * nc + core) * row_count + jnp.arange(row_count, dtype=jnp.int32)
    keep = (positions < lengths[0])[:, None]
    inputs = spread_rows(jnp.where(keep, tokens_in[0], jnp.zeros_like(tokens_in[0])))
    inputs = inputs.reshape(mine, size, block)
    upstream = spread_rows(jnp.where(keep, cotangent[0], jnp.zeros_like(cotangent[0])))
    upstream = upstream.reshape(mine, size, block)

    factors = jnp.concatenate([time_blocks, spectral_blocks], axis=0).reshape(-1, 128)
    factors = jnp.broadcast_to(factors[None], (2 * ny,) + factors.shape)
    factors = lax.all_to_all(factors, ("section", "y"), 0, 0, tiled=True)
    factors = factors.reshape(2, ny, 2, per, size, size)
    time_all = factors[:, :, 0].reshape(2, mine, size, size)
    spectral_all = factors[:, :, 1].reshape(2, mine, size, size)

    def sets_first(values, axis):
        shape = values.shape
        split = values.reshape(shape[:axis] + (ny, nc, per) + shape[axis + 1 :])
        split = jnp.moveaxis(split, axis + 1, axis)
        split = jnp.where(core == 0, split, jnp.flip(split, axis))
        return split.reshape(shape)

    def sets_back(values, axis):
        shape = values.shape
        split = values.reshape(shape[:axis] + (nc, ny, per) + shape[axis + 1 :])
        split = jnp.where(core == 0, split, jnp.flip(split, axis))
        return jnp.moveaxis(split, axis, axis + 1).reshape(shape)

    time_all = sets_first(time_all, 2)
    spectral_all = sets_first(spectral_all, 3)

    kernel = spectral_kernel[0].reshape(per, size, ny, block)
    kernel = jnp.transpose(kernel, (2, 0, 1, 3))
    kernel = jnp.concatenate([kernel, kernel], axis=0)
    kernel = lax.all_to_all(kernel, ("section", "y"), 0, 0, tiled=True)
    kernel_all = kernel.reshape(2, mine, size, block)

    own_mlp = jnp.concatenate(
        [
            lax.dynamic_index_in_dim(gate_weight[0], y, 0, keepdims=False).reshape(-1, block),
            lax.dynamic_index_in_dim(up_weight[0], y, 0, keepdims=False).reshape(-1, block),
            lax.dynamic_index_in_dim(down_weight[0], y, 0, keepdims=False),
        ]
    )
    halves = own_mlp.reshape(2, -1, block)
    got = section_swap(lax.dynamic_index_in_dim(halves, core, 0, keepdims=False))
    sibling = core_swap(got)
    other_mlp = jnp.where(core == 0, jnp.stack([got, sibling]), jnp.stack([sibling, got]))
    other_mlp = other_mlp.reshape(own_mlp.shape)

    hidden_units = down_weight.shape[2]

    def mlp_weights(packed):
        packed = packed.reshape(3, -1, block)
        return (
            packed[0].reshape(block, hidden_units),
            packed[1].reshape(block, hidden_units),
            packed[2],
        )

    mlp_all = [
        mlp_weights(jnp.where(first_layer, own_mlp, other_mlp)),
        mlp_weights(jnp.where(first_layer, other_mlp, own_mlp)),
    ]

    flat = (mine * size, block)
    cube = (mine, size, block)
    activations = inputs
    stash = []
    for layer in range(2):
        hidden, mix_saved = mixer_forward(
            time_all[layer], spectral_all[layer], kernel_all[layer], activations
        )
        hidden = hidden.reshape(flat)
        output, mlp_saved = mlp_forward(mlp_all[layer], hidden, width, layer == 0)
        stash.append((hidden, mix_saved, mlp_saved))
        if layer == 0:
            activations = output.reshape(cube)
    grads = [None, None]
    for layer in (1, 0):
        hidden, mix_saved, mlp_saved = stash[layer]
        grad_hidden, mlp_grad = mlp_backward(
            mlp_all[layer], hidden, mlp_saved, upstream.reshape(flat), width
        )
        upstream, mix_grads = mixer_backward(
            time_all[layer],
            spectral_all[layer],
            kernel_all[layer],
            mix_saved,
            grad_hidden.reshape(cube),
            layer == 1,
        )
        grads[layer] = mix_grads + (mlp_grad,)
    time_grad, spectral_grad, kernel_grad, mlp_grad = (
        jnp.where(first_layer, grads[0][member], grads[1][member]) for member in range(4)
    )

    piece = hidden_units // (ny * nc * nr)
    mlp_grad = mlp_grad.reshape(3, ny, nc, nr, piece, block)
    keep_half = lax.dynamic_index_in_dim(mlp_grad, core, 2, keepdims=False)
    send_half = lax.dynamic_index_in_dim(mlp_grad, 1 - core, 2, keepdims=False)
    mlp_grad = (keep_half.astype(F32) + core_swap(send_half).astype(F32)).astype(BF)
    mlp_grad = jnp.transpose(mlp_grad, (1, 2, 0, 3, 4)).reshape(ny * nr, 3, piece, block)
    mlp_grad = lax.all_to_all(mlp_grad, ("y", "rep"), 0, 0, tiled=True)
    mlp_grad = jnp.sum(mlp_grad.reshape(ny, nr, 3, piece, block).astype(F32), axis=1)
    part_gate = jnp.transpose(mlp_grad[:, 0], (0, 2, 1))
    part_up = jnp.transpose(mlp_grad[:, 1], (0, 2, 1))
    part_down = mlp_grad[:, 2]

    kernel_grad = kernel_grad.reshape(ny, per, size, 2, block // 2)
    kernel_grad = jnp.transpose(kernel_grad, (0, 3, 1, 2, 4)).reshape(nr, per, size, block // 2)
    kernel_grad = lax.all_to_all(kernel_grad, "rep", 0, 0, tiled=True)
    kernel_grad = jnp.sum(kernel_grad.astype(F32), axis=0).astype(BF)
    holders = [
        (k * nr + 2 * to + half, to * nr + 2 * k + half)
        for k in range(ny)
        for to in range(ny)
        for half in range(2)
    ]
    part_kernel = lax.ppermute(kernel_grad, ("y", "rep"), holders).astype(F32)

    time_grad = sets_back(time_grad, 1).reshape(ny, per, nr, size // nr, size)
    spectral_grad = sets_back(spectral_grad, 2).reshape(ny, per, nr, size // nr, size)
    factor_grad = jnp.stack([time_grad, spectral_grad])
    factor_grad = jnp.transpose(factor_grad, (1, 3, 0, 2, 4, 5)).reshape(ny * nr, -1, 128)
    factor_grad = lax.all_to_all(factor_grad, ("y", "rep"), 0, 0, tiled=True)
    factor_grad = jnp.sum(factor_grad.astype(F32), axis=0).reshape(2, per, size // nr, size)
    part_time, part_spectral = factor_grad[0], factor_grad[1]

    parts = (part_time, part_spectral, part_kernel, part_gate, part_up, part_down)
    squares = jnp.stack([jnp.sum(member * member) for member in parts])
    everyone = ny * nc * nr
    squares = jnp.broadcast_to(jnp.pad(squares, (0, 122))[None, None], (everyone, 1, 128))
    squares = lax.all_to_all(squares, ("y", "core", "rep"), 0, 0, tiled=True)
    square_totals = jnp.sum(squares, axis=(0, 1))
    counts = (
        time_blocks[0].size * ny * nc,
        spectral_blocks[0].size * ny * nc,
        spectral_kernel[0].size * ny * nc,
        gate_weight[0].size,
        up_weight[0].size,
        down_weight[0].size,
    )
    momenta = (
        momentum_time,
        momentum_spectral,
        momentum_kernel,
        momentum_gate,
        momentum_up,
        momentum_down,
    )
    results = []
    for member in range(6):
        inv_scale = lax.rsqrt(square_totals[member] / counts[member] + norm_eps)
        results.append((momentum_coef * momenta[member][0] + parts[member] * inv_scale)[None])
    return tuple(results)


def solution(mesh):
    sections, seqs, reps = (mesh.shape[name] for name in ("section", "seq", "rep"))
    split = Mesh(
        mesh.devices.reshape(sections, seqs // 2, 2, reps), ("section", "y", "core", "rep")
    )
    seq = ("y", "core")
    everyone = ("y", "core", "rep")
    placed = (
        P("rep", seq, None),
        P("rep"),
        P("rep", seq, None),
        P("section", seq, None, None),
        P("section", seq, None, None),
        P("section", seq, None, None),
        P("section", None, None, None),
        P("section", None, None, None),
        P("section", None, None, None),
        P("section", seq, "rep", None),
        P("section", seq, "rep", None),
        P("section", seq, None, "rep"),
        P("section", None, None, everyone),
        P("section", None, None, everyone),
        P("section", None, everyone, None),
    )
    return jax.shard_map(
        shards,
        mesh=split,
        in_specs=placed,
        out_specs=placed[9:],
        check_vma=False,
    )
```

```python
import functools

import jax
import jax.numpy as jnp
from jax import lax
from jax.experimental import pallas as pl
from jax.experimental.pallas import tpu as pltpu
from jax.sharding import Mesh
from jax.sharding import PartitionSpec as P

momentum_coef = 0.9
norm_eps = 1e-06
BF = jnp.bfloat16
F32 = jnp.float32


def product(pattern, first_operand, second_operand):
    return jnp.einsum(pattern, first_operand, second_operand, preferred_element_type=F32)


def core_swap(value):
    return lax.ppermute(value, "core", [(0, 1), (1, 0)])


def section_swap(value):
    return lax.ppermute(value, "section", [(0, 1), (1, 0)])


def sum_over_y(value):
    count = lax.axis_size("y")
    total = value
    for step in range(1, count):
        total = total + lax.ppermute(value, "y", [(i, (i + step) % count) for i in range(count)])
    return total


def time_mix_forward(time_mix, values):
    mixed = product("aij,ajc->iac", time_mix, values).astype(BF)
    half = mixed.shape[0] // 2
    return mixed[:half], mixed[half:]


def to_columns(time_mix, values):
    own, other = time_mix_forward(time_mix, values)
    return jnp.concatenate([own, core_swap(other)], axis=1)


def to_rows(blocks):
    half = blocks.shape[1] // 2
    own, other = blocks[:, :half], blocks[:, half:]
    return jnp.concatenate([own, core_swap(other)], axis=0)


def mixer_forward(time_mix, spectral_mix, kernel, inputs):
    columns = to_columns(time_mix, inputs)
    spectrum = product("bij,bjc->bic", spectral_mix, columns)
    weighted = (kernel.astype(F32) * spectrum).astype(BF)
    returned = product("bji,bjc->bic", spectral_mix, weighted).astype(BF)
    rows_back = to_rows(returned)
    mixed = product("aji,jac->aic", time_mix, rows_back)
    hidden = (inputs.astype(F32) + mixed).astype(BF)
    return hidden, (inputs, columns, spectrum, weighted, rows_back)


def mixer_backward(time_mix, spectral_mix, kernel, stored, grad_hidden, need_entry):
    inputs, columns, spectrum, weighted, rows_back = stored
    grad_mixed = grad_hidden.astype(BF)
    grad_cols = to_columns(time_mix, grad_mixed)
    time_grad = product("iac,ajc->aij", rows_back, grad_mixed)
    grad_weighted = product("bji,bic->bjc", spectral_mix, grad_cols)
    spectral_grad = product("bjc,bic->bji", weighted, grad_cols)
    kernel_grad = (grad_weighted * spectrum).astype(BF)
    grad_spectrum = (grad_weighted * kernel.astype(F32)).astype(BF)
    grad_columns = product("bij,bic->bjc", spectral_mix, grad_spectrum).astype(BF)
    spectral_grad = spectral_grad + product("bic,bjc->bij", grad_spectrum, columns)
    grad_rows = to_rows(grad_columns)
    time_grad = time_grad + product("iac,ajc->aij", grad_rows, inputs)
    entry = None
    if need_entry:
        entry = (grad_hidden + product("aij,iac->ajc", time_mix, grad_rows)).astype(BF)
    return entry, (time_grad, spectral_grad, kernel_grad)


def dot(first_operand, second_operand, dims=((1,), (0,))):
    return lax.dot_general(first_operand, second_operand, (dims, ((), ())), preferred_element_type=F32)


def sigmoid(value):
    return 0.5 * jnp.tanh(0.5 * value) + 0.5


def mlp_forward_kernel(chunk, normed_ref, hidden_ref, gate_ref, up_ref, down_ref, out_ref):
    normed = normed_ref[...]
    total = hidden_ref[...].astype(F32)
    for start in range(0, gate_ref.shape[1], chunk):
        part = slice(start, start + chunk)
        gate = dot(normed, gate_ref[:, part])
        upper = dot(normed, up_ref[:, part])
        active = (gate * sigmoid(gate) * upper).astype(BF)
        total = total + dot(active, down_ref[part, :])
    out_ref[...] = total.astype(BF)


def mlp_backward_kernel(
    chunk, normed_ref, cot_ref, gate_ref, up_ref, down_ref, active_ref, grad_gate_ref, grad_up_ref, out_ref
):
    normed, cot = normed_ref[...], cot_ref[...]
    total = None
    for start in range(0, gate_ref.shape[1], chunk):
        part = slice(start, start + chunk)
        gate = dot(normed, gate_ref[:, part])
        upper = dot(normed, up_ref[:, part])
        grad_active = dot(cot, down_ref[part, :], ((1,), (1,)))
        sigma = sigmoid(gate)
        silu = gate * sigma
        active_ref[:, part] = (silu * upper).astype(BF)
        grad_up = (grad_active * silu).astype(BF)
        grad_gate = (grad_active * upper * (sigma + silu * (1.0 - sigma))).astype(BF)
        grad_up_ref[:, part] = grad_up
        grad_gate_ref[:, part] = grad_gate
        term = dot(grad_gate, gate_ref[:, part], ((1,), (1,)))
        term = term + dot(grad_up, up_ref[:, part], ((1,), (1,)))
        total = term if total is None else total + term
    out_ref[...] = total


def row_specs(tile, *widths):
    return [pl.BlockSpec((tile, width), lambda i: (i, 0)) for width in widths]


def whole_specs(*arrays):
    return [pl.BlockSpec(array.shape, lambda i, n=array.ndim: (0,) * n) for array in arrays]


def mlp_forward(weights, normed, hidden):
    rows, block = normed.shape
    units = weights[0].shape[1]
    tile = min(512, rows)
    return pl.pallas_call(
        functools.partial(mlp_forward_kernel, min(256, units)),
        grid=(rows // tile,),
        in_specs=row_specs(tile, block, block) + whole_specs(*weights),
        out_specs=row_specs(tile, block)[0],
        out_shape=jax.ShapeDtypeStruct((rows, block), BF),
        compiler_params=pltpu.CompilerParams(vmem_limit_bytes=32 * 2**20),
        cost_estimate=pl.CostEstimate(
            flops=6 * rows * block * units,
            bytes_accessed=6 * rows * block + 6 * block * units,
            transcendentals=rows * units,
        ),
    )(normed, hidden, *weights)


def mlp_backward(weights, normed, cot):
    rows, block = normed.shape
    units = weights[0].shape[1]
    tile = min(512, rows)
    return pl.pallas_call(
        functools.partial(mlp_backward_kernel, min(256, units)),
        grid=(rows // tile,),
        in_specs=row_specs(tile, block, block) + whole_specs(*weights),
        out_specs=row_specs(tile, units, units, units, block),
        out_shape=[jax.ShapeDtypeStruct((rows, units), BF)] * 3
        + [jax.ShapeDtypeStruct((rows, block), F32)],
        compiler_params=pltpu.CompilerParams(vmem_limit_bytes=40 * 2**20),
        cost_estimate=pl.CostEstimate(
            flops=10 * rows * block * units,
            bytes_accessed=8 * rows * block + 6 * block * units + 6 * rows * units,
            transcendentals=rows * units,
        ),
    )(normed, cot, *weights)


def normalise(hidden, width):
    wide = hidden.astype(F32)
    inv_rms = lax.rsqrt(sum_over_y(jnp.sum(wide * wide, axis=-1)) / width + norm_eps)[..., None]
    return inv_rms, (wide * inv_rms).astype(BF)


def normalise_backward(hidden, inv_rms, upstream, grad_normed, width):
    wide = hidden.astype(F32)
    centred = sum_over_y(jnp.sum(grad_normed * wide, axis=-1))[..., None] / width
    return upstream.astype(F32) + inv_rms * grad_normed - wide * inv_rms**3 * centred


def mlp_weight_grads(normed, cot, active, grad_gate, grad_up):
    return (
        product("rf,rd->fd", grad_gate, normed).astype(BF),
        product("rf,rd->fd", grad_up, normed).astype(BF),
        product("rf,rd->fd", active, cot).astype(BF),
    )


def totals_kernel(factor_ref, kernel_ref, mlp_ref, sum_ref, square_ref):
    factor = jnp.sum(factor_ref[...].astype(F32), axis=0)
    sum_ref[...] = factor
    half = factor.shape[1] // 2
    lanes = lax.broadcasted_iota(jnp.int32, factor.shape, 1)
    squared = factor * factor
    kernel = kernel_ref[...].astype(F32)
    terms = [
        jnp.where(lanes < half, squared, 0.0),
        jnp.where(lanes < half, 0.0, squared),
        jnp.sum(kernel * kernel, axis=0),
    ]
    for member in range(mlp_ref.shape[0]):
        value = jnp.sum(mlp_ref[member] * mlp_ref[member], axis=0)
        terms.append(value)
    places = lax.broadcasted_iota(jnp.int32, square_ref.shape, 1)
    squares = jnp.zeros(square_ref.shape, F32)
    for member, term in enumerate(terms):
        squares = jnp.where(places == member, jnp.sum(term, axis=(0, 1), keepdims=True), squares)
    square_ref[...] = squares


def totals(factor, kernel, mlp):
    return pl.pallas_call(
        totals_kernel,
        out_shape=[
            jax.ShapeDtypeStruct(factor.shape[1:], F32),
            jax.ShapeDtypeStruct((1, 128), F32),
        ],
    )(factor, kernel, mlp)


def update_kernel(counts, square_ref, *refs):
    total = jnp.sum(square_ref[...], axis=0)
    members = len(counts)
    for member, count in enumerate(counts):
        inv_scale = lax.rsqrt(total[:, member : member + 1] / count + norm_eps)
        momentum, part, out = (refs[member + group * members] for group in range(3))
        value = part[...].astype(F32)
        scale = jnp.reshape(inv_scale, (1,) * value.ndim)
        out[...] = momentum_coef * momentum[...] + value * scale


def update(counts, squares, momenta, parts):
    return pl.pallas_call(
        functools.partial(update_kernel, counts),
        out_shape=[jax.ShapeDtypeStruct(momentum.shape, F32) for momentum in momenta],
    )(squares, *momenta, *parts)


def spread_rows(values):
    ny = lax.axis_size("y")
    rows, width = values.shape
    pieces = jnp.transpose(values.reshape(rows, ny, width // ny), (1, 0, 2))
    return lax.all_to_all(pieces, "y", 0, 0, tiled=True).reshape(ny * rows, width // ny)


def shards(
    tokens_in,
    lengths,
    cotangent,
    time_blocks,
    spectral_blocks,
    spectral_kernel,
    gate_weight,
    up_weight,
    down_weight,
    momentum_time,
    momentum_spectral,
    momentum_kernel,
    momentum_gate,
    momentum_up,
    momentum_down,
):
    ny, nc, nr = lax.axis_size("y"), lax.axis_size("core"), lax.axis_size("rep")
    section, y, core = lax.axis_index("section"), lax.axis_index("y"), lax.axis_index("core")
    _, row_count, width = tokens_in.shape
    block = width // ny
    per = time_blocks.shape[1]
    size = time_blocks.shape[2]
    mine = per * ny
    first_layer = section == 0

    positions = (y * nc + core) * row_count + jnp.arange(row_count, dtype=jnp.int32)
    keep = (positions < lengths[0])[:, None]
    inputs = spread_rows(jnp.where(keep, tokens_in[0], jnp.zeros_like(tokens_in[0])))
    inputs = inputs.reshape(mine, size, block)
    upstream = spread_rows(jnp.where(keep, cotangent[0], jnp.zeros_like(cotangent[0])))
    upstream = upstream.reshape(mine, size, block)

    factors = jnp.concatenate([time_blocks, spectral_blocks], axis=-1)
    factors = jnp.broadcast_to(factors, (2 * ny,) + factors.shape[1:])
    factors = lax.all_to_all(factors, ("section", "y"), 0, 0, tiled=True)
    factors = factors.reshape(2, mine, size, 2 * size)
    time_all, spectral_all = factors[..., :size], factors[..., size:]

    def sets_first(values, axis):
        shape = values.shape
        split = values.reshape(shape[:axis] + (ny, nc, per) + shape[axis + 1 :])
        split = jnp.moveaxis(split, axis + 1, axis)
        split = jnp.where(core == 0, split, jnp.flip(split, axis))
        return split.reshape(shape)

    def sets_back(values, axis):
        shape = values.shape
        split = values.reshape(shape[:axis] + (nc, ny, per) + shape[axis + 1 :])
        split = jnp.where(core == 0, split, jnp.flip(split, axis))
        return jnp.moveaxis(split, axis, axis + 1).reshape(shape)

    time_all = sets_first(time_all, 2)
    spectral_all = sets_first(spectral_all, 3)

    own_kernel = spread_rows(spectral_kernel[0].reshape(per * size, width))
    own_kernel = own_kernel.reshape(mine, size, block)
    other_kernel = section_swap(own_kernel)
    kernel_all = [
        jnp.where(first_layer, own_kernel, other_kernel),
        jnp.where(first_layer, other_kernel, own_kernel),
    ]

    own_mlp = [
        lax.dynamic_index_in_dim(weight[0], y, 0, keepdims=False)
        for weight in (gate_weight, up_weight, down_weight)
    ]
    got = [
        section_swap(lax.dynamic_index_in_dim(weight.reshape(2, -1, weight.shape[1]), core, 0, keepdims=False))
        for weight in own_mlp
    ]
    sibling = [core_swap(weight) for weight in got]
    other_mlp = [
        jnp.where(core == 0, jnp.concatenate([one, two]), jnp.concatenate([two, one]))
        for one, two in zip(got, sibling)
    ]
    mlp_all = [
        [jnp.where(first_layer, one, two) for one, two in zip(own_mlp, other_mlp)],
        [jnp.where(first_layer, two, one) for one, two in zip(own_mlp, other_mlp)],
    ]
    hidden_units = down_weight.shape[2]

    flat = (mine * size, block)
    cube = (mine, size, block)
    activations = inputs
    stash = []
    for layer in range(2):
        hidden, mix_saved = mixer_forward(
            time_all[layer], spectral_all[layer], kernel_all[layer], activations
        )
        hidden = hidden.reshape(flat)
        inv_rms, normed = normalise(hidden, width)
        stash.append((hidden, mix_saved, inv_rms, normed))
        if layer == 0:
            activations = mlp_forward(mlp_all[layer], normed, hidden).reshape(cube)
    grads = [None, None]
    for layer in (1, 0):
        hidden, mix_saved, inv_rms, normed = stash[layer]
        cot = upstream.reshape(flat)
        active, grad_gate, grad_up, grad_normed = mlp_backward(mlp_all[layer], normed, cot)
        grad_hidden = normalise_backward(hidden, inv_rms, cot, grad_normed, width)
        mlp_grads = mlp_weight_grads(normed, cot, active, grad_gate, grad_up)
        upstream, mix_grads = mixer_backward(
            time_all[layer],
            spectral_all[layer],
            kernel_all[layer],
            mix_saved,
            grad_hidden.reshape(cube),
            layer == 1,
        )
        grads[layer] = mix_grads + mlp_grads
    time_grad, spectral_grad, kernel_grad, *mlp_grad = (
        jnp.where(first_layer, one, two) for one, two in zip(*grads)
    )

    piece = hidden_units // (ny * nc * nr)
    mlp_grad = jnp.stack(mlp_grad).reshape(3, ny, nc, nr, piece, block)
    keep_half = lax.dynamic_index_in_dim(mlp_grad, core, 2, keepdims=False)
    send_half = lax.dynamic_index_in_dim(mlp_grad, 1 - core, 2, keepdims=False)
    mlp_grad = (keep_half.astype(F32) + core_swap(send_half).astype(F32)).astype(BF)
    mlp_grad = jnp.transpose(mlp_grad, (1, 2, 0, 3, 4)).reshape(ny * nr, 3, piece, block)
    mlp_grad = lax.all_to_all(mlp_grad, ("y", "rep"), 0, 0, tiled=True)
    mlp_grad = jnp.sum(mlp_grad.reshape(ny, nr, 3, piece, block).astype(F32), axis=1)
    mlp_grad = jnp.transpose(mlp_grad, (1, 0, 2, 3)).reshape(3, ny * piece, block)

    kernel_grad = kernel_grad.reshape(ny, per, size, 2, block // 2)
    kernel_grad = jnp.transpose(kernel_grad, (0, 3, 1, 2, 4)).reshape(nr, per, size, block // 2)
    kernel_grad = lax.all_to_all(kernel_grad, "rep", 0, 0, tiled=True)
    kernel_grad = jnp.sum(kernel_grad.astype(F32), axis=0).astype(BF)
    holders = [
        (k * nr + 2 * to + half, to * nr + 2 * k + half)
        for k in range(ny)
        for to in range(ny)
        for half in range(2)
    ]
    part_kernel = lax.ppermute(kernel_grad, ("y", "rep"), holders)

    factor_grad = jnp.concatenate([sets_back(time_grad, 1), spectral_grad], axis=-1).astype(BF)
    factor_grad = factor_grad.reshape(ny, per, nr, size // nr, 2 * size)
    factor_grad = jnp.transpose(factor_grad, (0, 2, 1, 3, 4)).reshape(ny * nr, size, 2 * size)
    factor_grad = lax.all_to_all(factor_grad, ("y", "rep"), 0, 0, tiled=True)

    factor_sum, squares = totals(factor_grad, part_kernel.reshape(-1, size, 2 * size), mlp_grad.reshape(3, -1, 8, 128))
    everyone = ny * nc * nr
    squares = jnp.broadcast_to(squares[None], (everyone, 1, 128))
    squares = lax.all_to_all(squares, ("y", "core", "rep"), 0, 0, tiled=True)
    parts = (
        factor_sum[:, :size],
        sets_back(factor_sum[:, size:], 1),
        part_kernel,
        *(mlp_grad[member].reshape(ny, piece, block) for member in range(3)),
    )
    counts = (
        time_blocks[0].size * ny * nc,
        spectral_blocks[0].size * ny * nc,
        spectral_kernel[0].size * ny * nc,
        gate_weight[0].size,
        up_weight[0].size,
        down_weight[0].size,
    )
    momenta = (
        momentum_time.reshape(size, size),
        momentum_spectral.reshape(size, size),
        momentum_kernel[0],
        jnp.swapaxes(momentum_gate[0], 1, 2),
        jnp.swapaxes(momentum_up[0], 1, 2),
        momentum_down[0],
    )
    new = update(counts, squares, momenta, parts)
    return (
        new[0].reshape(momentum_time.shape),
        new[1].reshape(momentum_spectral.shape),
        new[2][None],
        jnp.swapaxes(new[3], 1, 2)[None],
        jnp.swapaxes(new[4], 1, 2)[None],
        new[5][None],
    )


def solution(mesh):
    sections, seqs, reps = (mesh.shape[name] for name in ("section", "seq", "rep"))
    split = Mesh(
        mesh.devices.reshape(sections, seqs // 2, 2, reps), ("section", "y", "core", "rep")
    )
    seq = ("y", "core")
    everyone = ("y", "core", "rep")
    placed = (
        P("rep", seq, None),
        P("rep"),
        P("rep", seq, None),
        P("section", seq, None, None),
        P("section", seq, None, None),
        P("section", seq, None, None),
        P("section", None, None, None),
        P("section", None, None, None),
        P("section", None, None, None),
        P("section", seq, "rep", None),
        P("section", seq, "rep", None),
        P("section", seq, None, "rep"),
        P("section", None, None, everyone),
        P("section", None, None, everyone),
        P("section", None, everyone, None),
    )
    return jax.shard_map(
        shards,
        mesh=split,
        in_specs=placed,
        out_specs=placed[9:],
        check_vma=False,
    )
```

```python
import functools

import jax
import jax.numpy as jnp
from jax import lax
from jax.experimental import pallas as pl
from jax.experimental.pallas import tpu as pltpu
from jax.sharding import Mesh
from jax.sharding import PartitionSpec as P

momentum_coef = 0.9
norm_eps = 1e-06
BF = jnp.bfloat16
F32 = jnp.float32


def product(pattern, first_operand, second_operand):
    return jnp.einsum(pattern, first_operand, second_operand, preferred_element_type=F32)


def core_swap(value):
    return lax.ppermute(value, "core", [(0, 1), (1, 0)])


def section_swap(value):
    return lax.ppermute(value, "section", [(0, 1), (1, 0)])


def sum_over_y(value):
    count = lax.axis_size("y")
    total = value
    for step in range(1, count):
        moved = lax.ppermute(value, "y", [(i, (i + step) % count) for i in range(count)])
        total = total + jnp.roll(moved, step * (value.shape[0] // count))
    return total


def time_mix_forward(time_mix, values):
    mixed = product("aij,ajc->iac", time_mix, values).astype(BF)
    half = mixed.shape[0] // 2
    return mixed[:half], mixed[half:]


def to_columns(time_mix, values):
    own, other = time_mix_forward(time_mix, values)
    return jnp.concatenate([own, core_swap(other)], axis=1)


def to_rows(blocks):
    half = blocks.shape[1] // 2
    own, other = blocks[:, :half], blocks[:, half:]
    return jnp.concatenate([own, core_swap(other)], axis=0)


def mixer_forward(time_mix, spectral_mix, kernel, inputs):
    columns = to_columns(time_mix, inputs)
    spectrum = product("bij,bjc->bic", spectral_mix, columns)
    weighted = (kernel.astype(F32) * spectrum).astype(BF)
    returned = product("bji,bjc->bic", spectral_mix, weighted).astype(BF)
    rows_back = to_rows(returned)
    mixed = product("aji,jac->aic", time_mix, rows_back)
    hidden = (inputs.astype(F32) + mixed).astype(BF)
    return hidden, (inputs, columns, spectrum.astype(BF), weighted, rows_back)


def mixer_backward(time_mix, spectral_mix, kernel, stored, grad_hidden, need_entry):
    inputs, columns, spectrum, weighted, rows_back = stored
    grad_mixed = grad_hidden.astype(BF)
    grad_cols = to_columns(time_mix, grad_mixed)
    time_grad = product("iac,ajc->aij", rows_back, grad_mixed)
    grad_weighted = product("bji,bic->bjc", spectral_mix, grad_cols)
    spectral_grad = product("bjc,bic->bji", weighted, grad_cols)
    kernel_grad = (grad_weighted * spectrum.astype(F32)).astype(BF)
    grad_spectrum = (grad_weighted * kernel.astype(F32)).astype(BF)
    grad_columns = product("bij,bic->bjc", spectral_mix, grad_spectrum).astype(BF)
    spectral_grad = spectral_grad + product("bic,bjc->bij", grad_spectrum, columns)
    grad_rows = to_rows(grad_columns)
    time_grad = time_grad + product("iac,ajc->aij", grad_rows, inputs)
    entry = None
    if need_entry:
        entry = (grad_hidden + product("aij,iac->ajc", time_mix, grad_rows)).astype(BF)
    return entry, (time_grad, spectral_grad, kernel_grad)


def dot(first_operand, second_operand, dims=((1,), (0,))):
    return lax.dot_general(first_operand, second_operand, (dims, ((), ())), preferred_element_type=F32)


def sigmoid(value):
    return 0.5 * jnp.tanh(0.5 * value) + 0.5


def mlp_forward_kernel(chunk, normed_ref, hidden_ref, gate_ref, up_ref, down_ref, out_ref):
    normed = normed_ref[...]
    total = hidden_ref[...].astype(F32)
    for start in range(0, gate_ref.shape[1], chunk):
        part = slice(start, start + chunk)
        gate = dot(normed, gate_ref[:, part])
        upper = dot(normed, up_ref[:, part])
        active = (gate * sigmoid(gate) * upper).astype(BF)
        total = total + dot(active, down_ref[part, :])
    out_ref[...] = total.astype(BF)


def mlp_backward_kernel(
    chunk, normed_ref, cot_ref, gate_ref, up_ref, down_ref, active_ref, grad_gate_ref, grad_up_ref, out_ref
):
    normed, cot = normed_ref[...], cot_ref[...]
    total = None
    for start in range(0, gate_ref.shape[1], chunk):
        part = slice(start, start + chunk)
        gate = dot(normed, gate_ref[:, part])
        upper = dot(normed, up_ref[:, part])
        grad_active = dot(cot, down_ref[part, :], ((1,), (1,)))
        sigma = sigmoid(gate)
        silu = gate * sigma
        active_ref[:, part] = (silu * upper).astype(BF)
        grad_up = (grad_active * silu).astype(BF)
        grad_gate = (grad_active * upper * (sigma + silu * (1.0 - sigma))).astype(BF)
        grad_up_ref[:, part] = grad_up
        grad_gate_ref[:, part] = grad_gate
        term = dot(grad_gate, gate_ref[:, part], ((1,), (1,)))
        term = term + dot(grad_up, up_ref[:, part], ((1,), (1,)))
        total = term if total is None else total + term
    out_ref[...] = total


def row_specs(tile, *widths):
    return [pl.BlockSpec((tile, width), lambda i: (i, 0)) for width in widths]


def whole_specs(*arrays):
    return [pl.BlockSpec(array.shape, lambda i, n=array.ndim: (0,) * n) for array in arrays]


def mlp_forward(weights, normed, hidden):
    rows, block = normed.shape
    units = weights[0].shape[1]
    tile = min(512, rows)
    return pl.pallas_call(
        functools.partial(mlp_forward_kernel, min(256, units)),
        grid=(rows // tile,),
        in_specs=row_specs(tile, block, block) + whole_specs(*weights),
        out_specs=row_specs(tile, block)[0],
        out_shape=jax.ShapeDtypeStruct((rows, block), BF),
        compiler_params=pltpu.CompilerParams(vmem_limit_bytes=32 * 2**20),
        cost_estimate=pl.CostEstimate(
            flops=6 * rows * block * units,
            bytes_accessed=6 * rows * block + 6 * block * units,
            transcendentals=rows * units,
        ),
    )(normed, hidden, *weights)


def mlp_backward(weights, normed, cot):
    rows, block = normed.shape
    units = weights[0].shape[1]
    tile = min(512, rows)
    return pl.pallas_call(
        functools.partial(mlp_backward_kernel, min(256, units)),
        grid=(rows // tile,),
        in_specs=row_specs(tile, block, block) + whole_specs(*weights),
        out_specs=row_specs(tile, units, units, units, block),
        out_shape=[jax.ShapeDtypeStruct((rows, units), BF)] * 3
        + [jax.ShapeDtypeStruct((rows, block), F32)],
        compiler_params=pltpu.CompilerParams(vmem_limit_bytes=40 * 2**20),
        cost_estimate=pl.CostEstimate(
            flops=10 * rows * block * units,
            bytes_accessed=8 * rows * block + 6 * block * units + 6 * rows * units,
            transcendentals=rows * units,
        ),
    )(normed, cot, *weights)


def normalise(hidden, width):
    wide = hidden.astype(F32)
    inv_rms = lax.rsqrt(sum_over_y(jnp.sum(wide * wide, axis=-1)) / width + norm_eps)[..., None]
    return inv_rms, (wide * inv_rms).astype(BF)


def normalise_backward(hidden, inv_rms, upstream, grad_normed, width):
    wide = hidden.astype(F32)
    centred = sum_over_y(jnp.sum(grad_normed * wide, axis=-1))[..., None] / width
    return upstream.astype(F32) + inv_rms * grad_normed - wide * inv_rms**3 * centred


def mlp_weight_grads(normed, cot, active, grad_gate, grad_up):
    return (
        product("rf,rd->fd", grad_gate, normed).astype(BF),
        product("rf,rd->fd", grad_up, normed).astype(BF),
        product("rf,rd->fd", active, cot).astype(BF),
    )


def pack_kernel(ny, per, place_ref, *refs):
    time_refs, spectral_refs, out_ref = refs[:2], refs[2:4], refs[4]
    section, y, core = place_ref[0], place_ref[1], place_ref[2]
    size = time_refs[0].shape[1]
    q = lax.broadcasted_iota(jnp.int32, (size, size), 0)
    a = lax.broadcasted_iota(jnp.int32, (size, size), 1)
    back, sib = (q // per) % ny, q // (per * ny)
    natural = lax.rem(y + ny - back, ny) * (2 * per) + (core ^ sib) * per + q % per
    order = (natural == a).astype(BF)

    def load(pair, rows, start):
        picked = [ref[pl.ds(rows * per, per), pl.ds(pl.multiple_of(start, per), per), :] for ref in pair]
        value = jnp.where(section == 0, picked[0], picked[1])
        return value.reshape(per * per, size)

    for to in range(ny):
        rows = lax.rem(y + ny - to, ny)
        for rep in range(2 * ny):
            from_y, from_core = rep // 2, rep % 2
            group = (core ^ from_core) * ny + lax.rem(y + ny - from_y, ny)
            time = load(time_refs, rows, group * per)
            spectral = dot(load(spectral_refs, rows, rep * per).astype(BF), order)
            out_ref[to * 2 * ny + rep] = jnp.concatenate([time, spectral], axis=1).astype(BF)


def pack_factors(ny, per, place, time_grads, spectral_grads):
    size = time_grads[0].shape[1]
    return pl.pallas_call(
        functools.partial(pack_kernel, ny, per),
        in_specs=[pl.BlockSpec(memory_space=pltpu.SMEM)] + [pl.BlockSpec(memory_space=pltpu.VMEM)] * 4,
        out_shape=jax.ShapeDtypeStruct((ny * 2 * ny, per * per, 2 * size), BF),
        compiler_params=pltpu.CompilerParams(vmem_limit_bytes=24 * 2**20),
    )(place, *time_grads, *spectral_grads)


def totals_kernel(factor_ref, kernel_ref, mlp_ref, sum_ref, square_ref):
    factor = jnp.sum(factor_ref[...].astype(F32), axis=0)
    sum_ref[...] = factor
    half = factor.shape[1] // 2
    lanes = lax.broadcasted_iota(jnp.int32, factor.shape, 1)
    squared = factor * factor
    kernel = kernel_ref[...].astype(F32)
    terms = [
        jnp.where(lanes < half, squared, 0.0),
        jnp.where(lanes < half, 0.0, squared),
        jnp.sum(kernel * kernel, axis=0),
    ]
    for member in range(mlp_ref.shape[0]):
        value = jnp.sum(mlp_ref[member] * mlp_ref[member], axis=0)
        terms.append(value)
    places = lax.broadcasted_iota(jnp.int32, square_ref.shape[1:], 1)
    squares = jnp.zeros(square_ref.shape[1:], F32)
    for member, term in enumerate(terms):
        squares = jnp.where(places == member, jnp.sum(term, axis=(0, 1), keepdims=True), squares)
    square_ref[...] = jnp.broadcast_to(squares[None], square_ref.shape)


def totals(copies, factor, kernel, mlp):
    return pl.pallas_call(
        totals_kernel,
        out_shape=[
            jax.ShapeDtypeStruct(factor.shape[1:], F32),
            jax.ShapeDtypeStruct((copies, 1, 128), F32),
        ],
    )(factor, kernel, mlp)


def update_kernel(counts, square_ref, *refs):
    total = jnp.sum(square_ref[...], axis=0)
    members = len(counts)
    for member, count in enumerate(counts):
        inv_scale = lax.rsqrt(total[:, member : member + 1] / count + norm_eps)
        momentum, part, out = (refs[member + group * members] for group in range(3))
        value = part[...].astype(F32)
        scale = jnp.reshape(inv_scale, (1,) * value.ndim)
        out[...] = momentum_coef * momentum[...] + value * scale


def update(counts, squares, momenta, parts):
    return pl.pallas_call(
        functools.partial(update_kernel, counts),
        out_shape=[jax.ShapeDtypeStruct(momentum.shape, F32) for momentum in momenta],
    )(squares, *momenta, *parts)


def gather_over_y(sent, own):
    count = lax.axis_size("y")
    moved = [
        lax.ppermute(sent(step), "y", [(i, (i + step) % count) for i in range(count)])
        for step in range(1, count)
    ]
    return [own] + moved


def spread_rows(values):
    count, y = lax.axis_size("y"), lax.axis_index("y")
    block = values.shape[1] // count

    def piece(step):
        return lax.dynamic_slice_in_dim(values, ((y + step) % count) * block, block, 1)

    return gather_over_y(piece, piece(0))


def barrier(*values):
    return lax.optimization_barrier(values)


def shards(
    tokens_in,
    lengths,
    cotangent,
    time_blocks,
    spectral_blocks,
    spectral_kernel,
    gate_weight,
    up_weight,
    down_weight,
    momentum_time,
    momentum_spectral,
    momentum_kernel,
    momentum_gate,
    momentum_up,
    momentum_down,
):
    ny, nc, nr = lax.axis_size("y"), lax.axis_size("core"), lax.axis_size("rep")
    section, y, core = lax.axis_index("section"), lax.axis_index("y"), lax.axis_index("core")
    _, row_count, width = tokens_in.shape
    block = width // ny
    per = time_blocks.shape[1]
    size = time_blocks.shape[2]
    mine = per * ny
    first_layer = section == 0

    flat = (mine * size, block)
    cube = (mine, size, block)

    place = jnp.arange(size, dtype=jnp.int32)
    from_core = core ^ (place // (ny * per))
    from_y = (y - place // per) % ny
    natural = from_y * (nc * per) + from_core * per + place % per
    order = (natural[:, None] == place[None, :]).astype(BF)

    own_kernel = spread_rows(spectral_kernel[0].reshape(per * size, width))
    factors = jnp.concatenate([time_blocks[0], spectral_blocks[0]], axis=-1)
    other_factors = section_swap(factors)

    own_mlp = [
        lax.dynamic_index_in_dim(weight[0], y, 0, keepdims=False)
        for weight in (gate_weight, up_weight, down_weight)
    ]
    hidden_units = down_weight.shape[2]
    half = hidden_units // 2
    sent = [
        lax.dynamic_slice_in_dim(weight, core * half, half, axis)
        for weight, axis in zip(own_mlp, (1, 1, 0))
    ]
    got = [section_swap(jnp.concatenate(sent[:2])), section_swap(sent[2])]

    factors = jnp.where(
        first_layer, jnp.stack([factors, other_factors]), jnp.stack([other_factors, factors])
    )
    own_kernel = jnp.concatenate(own_kernel).reshape(cube)
    other_kernel = section_swap(own_kernel)
    own_kernel, factors, tokens = barrier(own_kernel, factors, tokens_in[0])
    factors = jnp.concatenate(gather_over_y(lambda step: factors, factors), axis=1)
    time_all = product("qi,laij->laqj", order, factors[..., :size]).astype(BF)
    spectral_all = product("lbia,qa->lbiq", factors[..., size:], order).astype(BF)

    positions = (y * nc + core) * row_count + jnp.arange(row_count, dtype=jnp.int32)
    keep = (positions < lengths[0])[:, None]
    inputs = jnp.concatenate(spread_rows(jnp.where(keep, tokens, jnp.zeros_like(tokens))))
    inputs = inputs.reshape(cube)

    inputs, seed = barrier(inputs, cotangent[0])
    upstream = spread_rows(jnp.where(keep, seed, jnp.zeros_like(seed)))
    *upstream, other_kernel = barrier(*upstream, other_kernel)
    upstream = jnp.concatenate(upstream)

    kernel_all = [
        jnp.where(first_layer, own_kernel, other_kernel),
        jnp.where(first_layer, other_kernel, own_kernel),
    ]

    sibling = [core_swap(weight) for weight in got]
    other_mlp = [
        jnp.concatenate([got[0][:block], sibling[0][:block]], axis=1),
        jnp.concatenate([got[0][block:], sibling[0][block:]], axis=1),
        jnp.concatenate([got[1], sibling[1]]),
    ]
    mlp_all = [
        [jnp.where(first_layer, one, two) for one, two in zip(own_mlp, other_mlp)],
        [jnp.where(first_layer, two, one) for one, two in zip(own_mlp, other_mlp)],
    ]

    activations = inputs
    stash = []
    for layer in range(2):
        hidden, mix_saved = mixer_forward(
            time_all[layer], spectral_all[layer], kernel_all[layer], activations
        )
        hidden = hidden.reshape(flat)
        inv_rms, normed = normalise(hidden, width)
        stash.append((hidden, mix_saved, inv_rms, normed))
        if layer == 0:
            activations = mlp_forward(mlp_all[layer], normed, hidden).reshape(cube)
    grads, time_grads, spectral_grads = [None, None], [None, None], [None, None]
    for layer in (1, 0):
        hidden, mix_saved, inv_rms, normed = stash[layer]
        cot = upstream.reshape(flat)
        active, grad_gate, grad_up, grad_normed = mlp_backward(mlp_all[layer], normed, cot)
        grad_hidden = normalise_backward(hidden, inv_rms, cot, grad_normed, width)
        mlp_grads = mlp_weight_grads(normed, cot, active, grad_gate, grad_up)
        grad_hidden, *mlp_grads = barrier(grad_hidden, *mlp_grads)
        upstream, mix_grads = mixer_backward(
            time_all[layer],
            spectral_all[layer],
            kernel_all[layer],
            mix_saved,
            grad_hidden.reshape(cube),
            layer == 1,
        )
        time_grads[layer], spectral_grads[layer], kernel_grad = mix_grads
        grads[layer] = (kernel_grad,) + tuple(mlp_grads)
    kernel_grad, *mlp_grad = (jnp.where(first_layer, one, two) for one, two in zip(*grads))

    piece = hidden_units // (ny * nc * nr)
    mlp_grad = jnp.stack(mlp_grad).reshape(3, ny, nc, nr, piece, block)
    keep_half = lax.dynamic_index_in_dim(mlp_grad, core, 2, keepdims=False)
    send_half = lax.dynamic_index_in_dim(mlp_grad, 1 - core, 2, keepdims=False)
    mlp_grad = (keep_half.astype(F32) + core_swap(send_half).astype(F32)).astype(BF)
    mlp_grad = jnp.transpose(mlp_grad, (1, 2, 0, 3, 4)).reshape(ny * nr, 3, piece, block)
    mlp_grad, kernel_grad = barrier(mlp_grad, kernel_grad)
    mlp_grad = lax.all_to_all(mlp_grad, ("y", "rep"), 0, 0, tiled=True)
    mlp_grad = jnp.sum(mlp_grad.reshape(ny, nr, 3, piece, block).astype(F32), axis=1)
    mlp_grad = jnp.transpose(mlp_grad, (1, 0, 2, 3)).reshape(3, ny * piece, block)

    kernel_grad = kernel_grad.reshape(ny, per, size, 2, block // 2)
    kernel_grad = jnp.transpose(kernel_grad, (0, 3, 1, 2, 4)).reshape(nr, per, size, block // 2)
    rep = lax.axis_index("rep")
    near = nr // 2

    def kernel_pieces(z):
        pieces = (z, z + near)
        return jnp.stack(
            [
                lax.dynamic_index_in_dim(
                    kernel_grad, ((y - piece // 2) % ny) * 2 + piece % 2, 0, keepdims=False
                )
                for piece in pieces
            ]
        )

    kernel_sum = kernel_pieces(rep % near).astype(F32)
    for flip in range(1, near):
        moved = lax.ppermute(
            kernel_pieces((rep % near) ^ flip), "rep", [(i, i ^ flip) for i in range(nr)]
        )
        kernel_sum = kernel_sum + moved.astype(F32)
    kernel_sum = kernel_sum.astype(BF)
    x = rep // near
    moved = lax.ppermute(
        lax.dynamic_index_in_dim(kernel_sum, 1 - x, 0, keepdims=False),
        "rep",
        [(i, i ^ near) for i in range(nr)],
    )
    kept = lax.dynamic_index_in_dim(kernel_sum, x, 0, keepdims=False)
    kernel_sum = (kept.astype(F32) + moved.astype(F32)).astype(BF)
    holders = [
        (k * nr + 2 * to + half, to * nr + 2 * k + half)
        for k in range(ny)
        for to in range(ny)
        for half in range(2)
    ]
    part_kernel = lax.ppermute(kernel_sum, ("y", "rep"), holders)

    place = jnp.stack([section, y, core]).astype(jnp.int32)
    factor_grad = pack_factors(ny, per, place, time_grads, spectral_grads)
    factor_grad, mlp_grad = barrier(factor_grad, mlp_grad)
    factor_grad = lax.all_to_all(factor_grad, ("y", "rep"), 0, 0, tiled=True)

    everyone = ny * nc * nr
    factor_sum, squares = totals(
        everyone, factor_grad, part_kernel.reshape(-1, size, 2 * size), mlp_grad.reshape(3, -1, 8, 128)
    )
    squares = lax.all_to_all(squares, ("y", "core", "rep"), 0, 0, tiled=True)
    parts = (
        factor_sum[:, :size],
        factor_sum[:, size:],
        part_kernel,
        *(mlp_grad[member].reshape(ny, piece, block) for member in range(3)),
    )
    counts = (
        time_blocks[0].size * ny * nc,
        spectral_blocks[0].size * ny * nc,
        spectral_kernel[0].size * ny * nc,
        gate_weight[0].size,
        up_weight[0].size,
        down_weight[0].size,
    )
    momenta = (
        momentum_time.reshape(size, size),
        momentum_spectral.reshape(size, size),
        momentum_kernel[0],
        jnp.swapaxes(momentum_gate[0], 1, 2),
        jnp.swapaxes(momentum_up[0], 1, 2),
        momentum_down[0],
    )
    new = update(counts, squares, momenta, parts)
    return (
        new[0].reshape(momentum_time.shape),
        new[1].reshape(momentum_spectral.shape),
        new[2][None],
        jnp.swapaxes(new[3], 1, 2)[None],
        jnp.swapaxes(new[4], 1, 2)[None],
        new[5][None],
    )


def solution(mesh):
    sections, seqs, reps = (mesh.shape[name] for name in ("section", "seq", "rep"))
    split = Mesh(
        mesh.devices.reshape(sections, seqs // 2, 2, reps), ("section", "y", "core", "rep")
    )
    seq = ("y", "core")
    everyone = ("y", "core", "rep")
    placed = (
        P("rep", seq, None),
        P("rep"),
        P("rep", seq, None),
        P("section", seq, None, None),
        P("section", seq, None, None),
        P("section", seq, None, None),
        P("section", None, None, None),
        P("section", None, None, None),
        P("section", None, None, None),
        P("section", seq, "rep", None),
        P("section", seq, "rep", None),
        P("section", seq, None, "rep"),
        P("section", None, None, everyone),
        P("section", None, None, everyone),
        P("section", None, everyone, None),
    )
    return jax.shard_map(
        shards,
        mesh=split,
        in_specs=placed,
        out_specs=placed[9:],
        check_vma=False,
    )
```

```python
import functools

import jax
import jax.numpy as jnp
from jax import lax
from jax.experimental import pallas as pl
from jax.experimental.pallas import tpu as pltpu
from jax.sharding import Mesh
from jax.sharding import PartitionSpec as P

momentum_coef = 0.9
norm_eps = 1e-06
BF = jnp.bfloat16
F32 = jnp.float32


def product(pattern, first_operand, second_operand):
    return jnp.einsum(pattern, first_operand, second_operand, preferred_element_type=F32)


def core_swap(value):
    return lax.ppermute(value, "core", [(0, 1), (1, 0)])


def section_swap(value):
    return lax.ppermute(value, "section", [(0, 1), (1, 0)])


def sum_over_y(value):
    count = lax.axis_size("y")
    total = value
    for step in range(1, count):
        moved = lax.ppermute(value, "y", [(i, (i + step) % count) for i in range(count)])
        total = total + jnp.roll(moved, step * (value.shape[0] // count))
    return total


def time_mix_forward(time_mix, values):
    mixed = product("aij,ajc->iac", time_mix, values).astype(BF)
    half = mixed.shape[0] // 2
    return mixed[:half], mixed[half:]


def to_columns(time_mix, values):
    own, other = time_mix_forward(time_mix, values)
    return jnp.concatenate([own, core_swap(other)], axis=1)


def to_rows(blocks):
    half = blocks.shape[1] // 2
    own, other = blocks[:, :half], blocks[:, half:]
    return jnp.concatenate([own, core_swap(other)], axis=0)


def mixer_forward(time_mix, spectral_mix, kernel, inputs):
    columns = to_columns(time_mix, inputs)
    spectrum = product("bij,bjc->bic", spectral_mix, columns)
    weighted = (kernel.astype(F32) * spectrum).astype(BF)
    returned = product("bji,bjc->bic", spectral_mix, weighted).astype(BF)
    rows_back = to_rows(returned)
    mixed = product("aji,jac->aic", time_mix, rows_back)
    hidden = (inputs.astype(F32) + mixed).astype(BF)
    return hidden, (inputs, columns, spectrum.astype(BF), weighted, rows_back)


def mixer_backward(time_mix, spectral_mix, kernel, stored, grad_hidden, sent):
    inputs, columns, spectrum, weighted, rows_back = stored
    grad_mixed = grad_hidden.astype(BF)
    grad_cols = to_columns(time_mix, grad_mixed)
    if sent is not None:
        sent, grad_cols = barrier(sent, grad_cols)
        sent = lax.all_to_all(sent, ("y", "rep"), 0, 0, tiled=True)
    time_grad = product("iac,ajc->aij", rows_back, grad_mixed)
    grad_weighted = product("bji,bic->bjc", spectral_mix, grad_cols)
    spectral_grad = product("bjc,bic->bji", weighted, grad_cols)
    kernel_grad = (grad_weighted * spectrum.astype(F32)).astype(BF)
    grad_spectrum = (grad_weighted * kernel.astype(F32)).astype(BF)
    grad_columns = product("bij,bic->bjc", spectral_mix, grad_spectrum).astype(BF)
    spectral_grad = spectral_grad + product("bic,bjc->bij", grad_spectrum, columns)
    grad_rows = to_rows(grad_columns)
    if sent is not None:
        sent, grad_rows = barrier(sent, grad_rows)
    time_grad = time_grad + product("iac,ajc->aij", grad_rows, inputs)
    entry = None
    if sent is None:
        entry = (grad_hidden + product("aij,iac->ajc", time_mix, grad_rows)).astype(BF)
    return entry, (time_grad, spectral_grad, kernel_grad), sent


def dot(first_operand, second_operand, dims=((1,), (0,))):
    return lax.dot_general(first_operand, second_operand, (dims, ((), ())), preferred_element_type=F32)


def sigmoid(value):
    return 0.5 * jnp.tanh(0.5 * value) + 0.5


def mlp_forward_kernel(chunk, normed_ref, hidden_ref, gate_ref, up_ref, down_ref, out_ref):
    normed = normed_ref[...]
    total = hidden_ref[...].astype(F32)
    for start in range(0, gate_ref.shape[1], chunk):
        part = slice(start, start + chunk)
        gate = dot(normed, gate_ref[:, part])
        upper = dot(normed, up_ref[:, part])
        active = (gate * sigmoid(gate) * upper).astype(BF)
        total = total + dot(active, down_ref[part, :])
    out_ref[...] = total.astype(BF)


def mlp_backward_kernel(
    chunk, normed_ref, cot_ref, gate_ref, up_ref, down_ref, active_ref, grad_gate_ref, grad_up_ref, out_ref
):
    normed, cot = normed_ref[...], cot_ref[...]
    total = None
    for start in range(0, gate_ref.shape[1], chunk):
        part = slice(start, start + chunk)
        gate = dot(normed, gate_ref[:, part])
        upper = dot(normed, up_ref[:, part])
        grad_active = dot(cot, down_ref[part, :], ((1,), (1,)))
        sigma = sigmoid(gate)
        silu = gate * sigma
        active_ref[:, part] = (silu * upper).astype(BF)
        grad_up = (grad_active * silu).astype(BF)
        grad_gate = (grad_active * upper * (sigma + silu * (1.0 - sigma))).astype(BF)
        grad_up_ref[:, part] = grad_up
        grad_gate_ref[:, part] = grad_gate
        term = dot(grad_gate, gate_ref[:, part], ((1,), (1,)))
        term = term + dot(grad_up, up_ref[:, part], ((1,), (1,)))
        total = term if total is None else total + term
    out_ref[...] = total


def row_specs(tile, *widths):
    return [pl.BlockSpec((tile, width), lambda i: (i, 0)) for width in widths]


def whole_specs(*arrays):
    return [pl.BlockSpec(array.shape, lambda i, n=array.ndim: (0,) * n) for array in arrays]


def mlp_forward(weights, normed, hidden):
    rows, block = normed.shape
    units = weights[0].shape[1]
    tile = min(512, rows)
    return pl.pallas_call(
        functools.partial(mlp_forward_kernel, min(256, units)),
        grid=(rows // tile,),
        in_specs=row_specs(tile, block, block) + whole_specs(*weights),
        out_specs=row_specs(tile, block)[0],
        out_shape=jax.ShapeDtypeStruct((rows, block), BF),
        compiler_params=pltpu.CompilerParams(vmem_limit_bytes=32 * 2**20),
        cost_estimate=pl.CostEstimate(
            flops=6 * rows * block * units,
            bytes_accessed=6 * rows * block + 6 * block * units,
            transcendentals=rows * units,
        ),
    )(normed, hidden, *weights)


def mlp_backward(weights, normed, cot):
    rows, block = normed.shape
    units = weights[0].shape[1]
    tile = min(512, rows)
    return pl.pallas_call(
        functools.partial(mlp_backward_kernel, min(256, units)),
        grid=(rows // tile,),
        in_specs=row_specs(tile, block, block) + whole_specs(*weights),
        out_specs=row_specs(tile, units, units, units, block),
        out_shape=[jax.ShapeDtypeStruct((rows, units), BF)] * 3
        + [jax.ShapeDtypeStruct((rows, block), F32)],
        compiler_params=pltpu.CompilerParams(vmem_limit_bytes=40 * 2**20),
        cost_estimate=pl.CostEstimate(
            flops=10 * rows * block * units,
            bytes_accessed=8 * rows * block + 6 * block * units + 6 * rows * units,
            transcendentals=rows * units,
        ),
    )(normed, cot, *weights)


def normalise(hidden, width):
    wide = hidden.astype(F32)
    inv_rms = lax.rsqrt(sum_over_y(jnp.sum(wide * wide, axis=-1)) / width + norm_eps)[..., None]
    return inv_rms, (wide * inv_rms).astype(BF)


def normalise_backward(hidden, inv_rms, upstream, grad_normed, width):
    wide = hidden.astype(F32)
    centred = sum_over_y(jnp.sum(grad_normed * wide, axis=-1))[..., None] / width
    return upstream.astype(F32) + inv_rms * grad_normed - wide * inv_rms**3 * centred


def mlp_weight_grads(normed, cot, active, grad_gate, grad_up):
    return (
        product("rf,rd->fd", grad_gate, normed).astype(BF),
        product("rf,rd->fd", grad_up, normed).astype(BF),
        product("rf,rd->fd", active, cot).astype(BF),
    )


def pack_kernel(ny, per, place_ref, *refs):
    time_refs, spectral_refs, out_ref = refs[:2], refs[2:4], refs[4]
    section, y, core = place_ref[0], place_ref[1], place_ref[2]
    size = time_refs[0].shape[1]
    q = lax.broadcasted_iota(jnp.int32, (size, size), 0)
    a = lax.broadcasted_iota(jnp.int32, (size, size), 1)
    back, sib = (q // per) % ny, q // (per * ny)
    natural = lax.rem(y + ny - back, ny) * (2 * per) + (core ^ sib) * per + q % per
    order = (natural == a).astype(BF)

    def load(pair, rows, start):
        picked = [ref[pl.ds(rows * per, per), pl.ds(pl.multiple_of(start, per), per), :] for ref in pair]
        value = jnp.where(section == 0, picked[0], picked[1])
        return value.reshape(per * per, size)

    for to in range(ny):
        rows = lax.rem(y + ny - to, ny)
        for rep in range(2 * ny):
            from_y, from_core = rep // 2, rep % 2
            group = (core ^ from_core) * ny + lax.rem(y + ny - from_y, ny)
            time = load(time_refs, rows, group * per)
            spectral = dot(load(spectral_refs, rows, rep * per).astype(BF), order)
            out_ref[to * 2 * ny + rep] = jnp.concatenate([time, spectral], axis=1).astype(BF)


def pack_factors(ny, per, place, time_grads, spectral_grads):
    size = time_grads[0].shape[1]
    return pl.pallas_call(
        functools.partial(pack_kernel, ny, per),
        in_specs=[pl.BlockSpec(memory_space=pltpu.SMEM)] + [pl.BlockSpec(memory_space=pltpu.VMEM)] * 4,
        out_shape=jax.ShapeDtypeStruct((ny * 2 * ny, per * per, 2 * size), BF),
        compiler_params=pltpu.CompilerParams(vmem_limit_bytes=24 * 2**20),
    )(place, *time_grads, *spectral_grads)


def totals_kernel(factor_ref, kernel_ref, mlp_ref, sum_ref, square_ref):
    factor = jnp.sum(factor_ref[...].astype(F32), axis=0)
    sum_ref[...] = factor
    half = factor.shape[1] // 2
    lanes = lax.broadcasted_iota(jnp.int32, factor.shape, 1)
    squared = factor * factor
    kernel = kernel_ref[...].astype(F32)
    terms = [
        jnp.where(lanes < half, squared, 0.0),
        jnp.where(lanes < half, 0.0, squared),
        jnp.sum(kernel * kernel, axis=0),
    ]
    for member in range(mlp_ref.shape[0]):
        value = jnp.sum(mlp_ref[member] * mlp_ref[member], axis=0)
        terms.append(value)
    places = lax.broadcasted_iota(jnp.int32, square_ref.shape[1:], 1)
    squares = jnp.zeros(square_ref.shape[1:], F32)
    for member, term in enumerate(terms):
        squares = jnp.where(places == member, jnp.sum(term, axis=(0, 1), keepdims=True), squares)
    square_ref[...] = jnp.broadcast_to(squares[None], square_ref.shape)


def totals(copies, factor, kernel, mlp):
    return pl.pallas_call(
        totals_kernel,
        out_shape=[
            jax.ShapeDtypeStruct(factor.shape[1:], F32),
            jax.ShapeDtypeStruct((copies, 1, 128), F32),
        ],
    )(factor, kernel, mlp)


def update_kernel(counts, square_ref, *refs):
    total = jnp.sum(square_ref[...], axis=0)
    members = len(counts)
    for member, count in enumerate(counts):
        inv_scale = lax.rsqrt(total[:, member : member + 1] / count + norm_eps)
        momentum, part, out = (refs[member + group * members] for group in range(3))
        value = part[...].astype(F32)
        scale = jnp.reshape(inv_scale, (1,) * value.ndim)
        out[...] = momentum_coef * momentum[...] + value * scale


def update(counts, squares, momenta, parts):
    return pl.pallas_call(
        functools.partial(update_kernel, counts),
        out_shape=[jax.ShapeDtypeStruct(momentum.shape, F32) for momentum in momenta],
    )(squares, *momenta, *parts)


def gather_over_y(sent, own):
    count = lax.axis_size("y")
    moved = [
        lax.ppermute(sent(step), "y", [(i, (i + step) % count) for i in range(count)])
        for step in range(1, count)
    ]
    return [own] + moved


def spread_rows(values):
    count, y = lax.axis_size("y"), lax.axis_index("y")
    block = values.shape[1] // count

    def piece(step):
        return lax.dynamic_slice_in_dim(values, ((y + step) % count) * block, block, 1)

    return gather_over_y(piece, piece(0))


def barrier(*values):
    return lax.optimization_barrier(values)


def shards(
    tokens_in,
    lengths,
    cotangent,
    time_blocks,
    spectral_blocks,
    spectral_kernel,
    gate_weight,
    up_weight,
    down_weight,
    momentum_time,
    momentum_spectral,
    momentum_kernel,
    momentum_gate,
    momentum_up,
    momentum_down,
):
    ny, nc, nr = lax.axis_size("y"), lax.axis_size("core"), lax.axis_size("rep")
    section, y, core = lax.axis_index("section"), lax.axis_index("y"), lax.axis_index("core")
    _, row_count, width = tokens_in.shape
    block = width // ny
    per = time_blocks.shape[1]
    size = time_blocks.shape[2]
    mine = per * ny
    first_layer = section == 0

    flat = (mine * size, block)
    cube = (mine, size, block)

    place = jnp.arange(size, dtype=jnp.int32)
    from_core = core ^ (place // (ny * per))
    from_y = (y - place // per) % ny
    natural = from_y * (nc * per) + from_core * per + place % per
    order = (natural[:, None] == place[None, :]).astype(BF)

    factors = jnp.concatenate([time_blocks[0], spectral_blocks[0]], axis=-1).reshape(-1, 2 * size)
    other_factors = section_swap(factors)
    own_kernel = spread_rows(spectral_kernel[0].reshape(per * size, width))

    own_mlp = [
        lax.dynamic_index_in_dim(weight[0], y, 0, keepdims=False)
        for weight in (gate_weight, up_weight, down_weight)
    ]
    hidden_units = down_weight.shape[2]
    half = hidden_units // 2
    sent = [
        lax.dynamic_slice_in_dim(weight, core * half, half, axis)
        for weight, axis in zip(own_mlp, (1, 1, 0))
    ]
    got = section_swap(jnp.concatenate(sent[:2] + [sent[2][:block], sent[2][block:]], axis=1))

    positions = (y * nc + core) * row_count + jnp.arange(row_count, dtype=jnp.int32)
    keep = (positions < lengths[0])[:, None]
    factors = jnp.concatenate(
        [
            jnp.where(first_layer, factors, other_factors),
            jnp.where(first_layer, other_factors, factors),
        ],
        axis=1,
    )
    own_kernel = jnp.concatenate(own_kernel).reshape(cube)
    own_kernel, factors, tokens, got = barrier(own_kernel, factors, tokens_in[0], got)
    other_kernel = section_swap(own_kernel)
    tokens = jnp.where(keep, tokens, jnp.zeros_like(tokens))

    def tokens_and_factors(step):
        piece = lax.dynamic_slice_in_dim(tokens, ((y + step) % ny) * block, block, 1)
        return jnp.concatenate([piece, factors])

    joined = gather_over_y(tokens_and_factors, tokens_and_factors(0))
    sibling = core_swap(got)
    other_mlp = [
        jnp.concatenate([got[:, :half], sibling[:, :half]], axis=1),
        jnp.concatenate([got[:, half : 2 * half], sibling[:, half : 2 * half]], axis=1),
        jnp.concatenate(
            [
                packed[:, 2 * half + start : 2 * half + start + block]
                for packed in (got, sibling)
                for start in (0, block)
            ]
        ),
    ]
    mlp_all = [
        [jnp.where(first_layer, one, two) for one, two in zip(own_mlp, other_mlp)],
        [jnp.where(first_layer, two, one) for one, two in zip(own_mlp, other_mlp)],
    ]
    inputs = jnp.concatenate([piece[:row_count] for piece in joined]).reshape(cube)
    factors = jnp.concatenate([piece[row_count:] for piece in joined]).reshape(mine, size, -1)
    time_all = [
        product("qi,aij->aqj", order, factors[..., start : start + size]).astype(BF)
        for start in (0, 2 * size)
    ]
    spectral_all = [
        product("bia,qa->biq", factors[..., start : start + size], order).astype(BF)
        for start in (size, 3 * size)
    ]
    weights = mlp_all[0] + mlp_all[1]
    inputs, seed, *weights = barrier(inputs, cotangent[0], *weights)
    mlp_all = [weights[:3], weights[3:]]
    upstream = spread_rows(jnp.where(keep, seed, jnp.zeros_like(seed)))
    kernel_all = [
        jnp.where(first_layer, own_kernel, other_kernel),
        jnp.where(first_layer, other_kernel, own_kernel),
    ]

    activations = inputs
    stash = []
    for layer in range(2):
        hidden, mix_saved = mixer_forward(
            time_all[layer], spectral_all[layer], kernel_all[layer], activations
        )
        hidden = hidden.reshape(flat)
        inv_rms, normed = normalise(hidden, width)
        stash.append((hidden, mix_saved, inv_rms, normed))
        if layer == 0:
            *upstream, normed = barrier(*upstream, normed)
            upstream = jnp.concatenate(upstream)
            activations = mlp_forward(mlp_all[layer], normed, hidden).reshape(cube)
    def reduce_mlp(layer_grads):
        picked = [jnp.where(first_layer, one, two) for one, two in zip(*layer_grads)]
        picked = jnp.stack(picked).reshape(3, ny, nc, nr, -1, block)
        keep_half = lax.dynamic_index_in_dim(picked, core, 2, keepdims=False)
        send_half = lax.dynamic_index_in_dim(picked, 1 - core, 2, keepdims=False)
        halves = (keep_half.astype(F32) + core_swap(send_half).astype(F32)).astype(BF)
        return jnp.transpose(halves, (1, 2, 0, 3, 4)).reshape(ny * nr, 3, -1, block)

    time_grads, spectral_grads, kernel_grads, mlp_grads = ([None, None] for _ in range(4))
    for layer in (1, 0):
        hidden, mix_saved, inv_rms, normed = stash[layer]
        cot = upstream.reshape(flat)
        active, grad_gate, grad_up, grad_normed = mlp_backward(mlp_all[layer], normed, cot)
        grad_hidden = normalise_backward(hidden, inv_rms, cot, grad_normed, width)
        mlp_grads[layer] = mlp_weight_grads(normed, cot, active, grad_gate, grad_up)
        grad_hidden, *mlp_grads[layer] = barrier(grad_hidden, *mlp_grads[layer])
        mlp_grad = reduce_mlp(mlp_grads) if layer == 0 else None
        upstream, mix_grads, mlp_grad = mixer_backward(
            time_all[layer],
            spectral_all[layer],
            kernel_all[layer],
            mix_saved,
            grad_hidden.reshape(cube),
            mlp_grad,
        )
        time_grads[layer], spectral_grads[layer], kernel_grads[layer] = mix_grads

    kernel_grad = jnp.where(first_layer, *kernel_grads)
    mlp_grad = jnp.sum(mlp_grad.reshape(ny, nr, 3, -1, block).astype(F32), axis=1)
    mlp_grad = jnp.transpose(mlp_grad, (1, 0, 2, 3)).reshape(3, -1, block)

    place = jnp.stack([section, y, core]).astype(jnp.int32)
    factor_grad = pack_factors(ny, per, place, time_grads, spectral_grads)

    rep = lax.axis_index("rep")
    near = nr // 2
    z = rep % near
    kernel_grad = kernel_grad.reshape(2, ny // 2, per * size, block)

    def kernel_pieces(to):
        start = (0, to // 2, 0, (to % 2) * (block // 2))
        return lax.dynamic_slice(kernel_grad, start, (2, 1, per * size, block // 2))[:, 0]

    moved = [
        lax.ppermute(kernel_pieces(z ^ flip), "rep", [(i, i ^ flip) for i in range(nr)])
        for flip in range(1, near)
    ]
    *moved, _ = barrier(*moved, factor_grad)
    kernel_sum = kernel_pieces(z).astype(F32)
    for piece in moved:
        kernel_sum = kernel_sum + piece.astype(F32)
    kernel_sum = kernel_sum.astype(BF)
    x = rep // near
    part_kernel = 0.0
    for turn in range(2):
        holders = [
            (k * nr + ((2 * back + side) ^ (near * turn)), ((k - back) % ny) * nr + 2 * k + side)
            for k in range(ny)
            for back in range(ny)
            for side in range(2)
        ]
        piece = lax.dynamic_index_in_dim(kernel_sum, x ^ turn, 0, keepdims=False)
        part_kernel = part_kernel + lax.ppermute(piece, ("y", "rep"), holders).astype(F32)
    part_kernel = part_kernel.reshape(per, size, block // 2)
    factor_grad = lax.all_to_all(factor_grad, ("y", "rep"), 0, 0, tiled=True)

    everyone = ny * nc * nr
    factor_sum, squares = totals(
        everyone, factor_grad, part_kernel.reshape(-1, size, 2 * size), mlp_grad.reshape(3, -1, 8, 128)
    )
    squares = lax.all_to_all(squares, ("y", "core", "rep"), 0, 0, tiled=True)
    parts = (
        factor_sum[:, :size],
        factor_sum[:, size:],
        part_kernel,
        *(mlp_grad[member].reshape(ny, -1, block) for member in range(3)),
    )
    counts = (
        time_blocks[0].size * ny * nc,
        spectral_blocks[0].size * ny * nc,
        spectral_kernel[0].size * ny * nc,
        gate_weight[0].size,
        up_weight[0].size,
        down_weight[0].size,
    )
    momenta = (
        momentum_time.reshape(size, size),
        momentum_spectral.reshape(size, size),
        momentum_kernel[0],
        jnp.swapaxes(momentum_gate[0], 1, 2),
        jnp.swapaxes(momentum_up[0], 1, 2),
        momentum_down[0],
    )
    new = update(counts, squares, momenta, parts)
    return (
        new[0].reshape(momentum_time.shape),
        new[1].reshape(momentum_spectral.shape),
        new[2][None],
        jnp.swapaxes(new[3], 1, 2)[None],
        jnp.swapaxes(new[4], 1, 2)[None],
        new[5][None],
    )


def solution(mesh):
    sections, seqs, reps = (mesh.shape[name] for name in ("section", "seq", "rep"))
    split = Mesh(
        mesh.devices.reshape(sections, seqs // 2, 2, reps), ("section", "y", "core", "rep")
    )
    seq = ("y", "core")
    everyone = ("y", "core", "rep")
    placed = (
        P("rep", seq, None),
        P("rep"),
        P("rep", seq, None),
        P("section", seq, None, None),
        P("section", seq, None, None),
        P("section", seq, None, None),
        P("section", None, None, None),
        P("section", None, None, None),
        P("section", None, None, None),
        P("section", seq, "rep", None),
        P("section", seq, "rep", None),
        P("section", seq, None, "rep"),
        P("section", None, None, everyone),
        P("section", None, None, everyone),
        P("section", None, everyone, None),
    )
    return jax.shard_map(
        shards,
        mesh=split,
        in_specs=placed,
        out_specs=placed[9:],
        check_vma=False,
    )
```

```python
import functools

import jax
import jax.numpy as jnp
from jax import lax
from jax.experimental import pallas as pl
from jax.experimental.pallas import tpu as pltpu
from jax.sharding import Mesh
from jax.sharding import PartitionSpec as P

momentum_coef = 0.9
norm_eps = 1e-06
BF = jnp.bfloat16
F32 = jnp.float32


def product(pattern, first_operand, second_operand):
    return jnp.einsum(pattern, first_operand, second_operand, preferred_element_type=F32)


def core_swap(value):
    return lax.ppermute(value, "core", [(0, 1), (1, 0)])


def section_swap(value):
    return lax.ppermute(value, "section", [(0, 1), (1, 0)])


def sum_over_y(value):
    count = lax.axis_size("y")
    total = value
    for step in range(1, count):
        moved = lax.ppermute(value, "y", [(i, (i + step) % count) for i in range(count)])
        total = total + jnp.roll(moved, step * (value.shape[0] // count))
    return total


def time_mix_forward(time_mix, values):
    mixed = product("aij,ajc->iac", time_mix, values).astype(BF)
    half = mixed.shape[0] // 2
    return mixed[:half], mixed[half:]


def to_columns(time_mix, values):
    own, other = time_mix_forward(time_mix, values)
    return jnp.concatenate([own, core_swap(other)], axis=1)


def to_rows(blocks):
    half = blocks.shape[1] // 2
    own, other = blocks[:, :half], blocks[:, half:]
    return jnp.concatenate([own, core_swap(other)], axis=0)


def mixer_forward(time_mix, spectral_mix, kernel, inputs):
    columns = to_columns(time_mix, inputs)
    spectrum = product("bij,bjc->bic", spectral_mix, columns)
    weighted = (kernel.astype(F32) * spectrum).astype(BF)
    returned = product("bji,bjc->bic", spectral_mix, weighted).astype(BF)
    rows_back = to_rows(returned)
    mixed = product("aji,jac->aic", time_mix, rows_back)
    hidden = (inputs.astype(F32) + mixed).astype(BF)
    return hidden, (inputs, columns, spectrum.astype(BF), weighted, rows_back)


def mixer_backward(time_mix, spectral_mix, kernel, stored, grad_hidden, sent):
    inputs, columns, spectrum, weighted, rows_back = stored
    grad_mixed = grad_hidden.astype(BF)
    grad_cols = to_columns(time_mix, grad_mixed)
    if sent is not None:
        sent, grad_cols = barrier(sent, grad_cols)
        sent = lax.all_to_all(sent, ("y", "rep"), 0, 0, tiled=True)
    time_grad = product("iac,ajc->aij", rows_back, grad_mixed)
    grad_weighted = product("bji,bic->bjc", spectral_mix, grad_cols)
    spectral_grad = product("bjc,bic->bji", weighted, grad_cols)
    kernel_grad = (grad_weighted * spectrum.astype(F32)).astype(BF)
    grad_spectrum = (grad_weighted * kernel.astype(F32)).astype(BF)
    grad_columns = product("bij,bic->bjc", spectral_mix, grad_spectrum).astype(BF)
    spectral_grad = spectral_grad + product("bic,bjc->bij", grad_spectrum, columns)
    grad_rows = to_rows(grad_columns)
    if sent is not None:
        sent, grad_rows = barrier(sent, grad_rows)
    time_grad = time_grad + product("iac,ajc->aij", grad_rows, inputs)
    entry = None
    if sent is None:
        entry = (grad_hidden + product("aij,iac->ajc", time_mix, grad_rows)).astype(BF)
    return entry, (time_grad, spectral_grad, kernel_grad), sent


def dot(first_operand, second_operand, dims=((1,), (0,))):
    return lax.dot_general(first_operand, second_operand, (dims, ((), ())), preferred_element_type=F32)


def sigmoid(value):
    return 0.5 * jnp.tanh(0.5 * value) + 0.5


def mlp_forward_kernel(chunk, normed_ref, hidden_ref, gate_ref, up_ref, down_ref, out_ref):
    normed = normed_ref[...]
    total = hidden_ref[...].astype(F32)
    for start in range(0, gate_ref.shape[1], chunk):
        part = slice(start, start + chunk)
        gate = dot(normed, gate_ref[:, part])
        upper = dot(normed, up_ref[:, part])
        active = (gate * sigmoid(gate) * upper).astype(BF)
        total = total + dot(active, down_ref[part, :])
    out_ref[...] = total.astype(BF)


def mlp_backward_kernel(
    chunk, normed_ref, cot_ref, gate_ref, up_ref, down_ref, active_ref, grad_gate_ref, grad_up_ref, out_ref
):
    normed, cot = normed_ref[...], cot_ref[...]
    total = None
    for start in range(0, gate_ref.shape[1], chunk):
        part = slice(start, start + chunk)
        gate = dot(normed, gate_ref[:, part])
        upper = dot(normed, up_ref[:, part])
        grad_active = dot(cot, down_ref[part, :], ((1,), (1,)))
        sigma = sigmoid(gate)
        silu = gate * sigma
        active_ref[:, part] = (silu * upper).astype(BF)
        grad_up = (grad_active * silu).astype(BF)
        grad_gate = (grad_active * upper * (sigma + silu * (1.0 - sigma))).astype(BF)
        grad_up_ref[:, part] = grad_up
        grad_gate_ref[:, part] = grad_gate
        term = dot(grad_gate, gate_ref[:, part], ((1,), (1,)))
        term = term + dot(grad_up, up_ref[:, part], ((1,), (1,)))
        total = term if total is None else total + term
    out_ref[...] = total


def row_specs(tile, *widths):
    return [pl.BlockSpec((tile, width), lambda i: (i, 0)) for width in widths]


def whole_specs(*arrays):
    return [pl.BlockSpec(array.shape, lambda i, n=array.ndim: (0,) * n) for array in arrays]


def mlp_forward(weights, normed, hidden):
    rows, block = normed.shape
    units = weights[0].shape[1]
    tile = min(512, rows)
    return pl.pallas_call(
        functools.partial(mlp_forward_kernel, min(256, units)),
        grid=(rows // tile,),
        in_specs=row_specs(tile, block, block) + whole_specs(*weights),
        out_specs=row_specs(tile, block)[0],
        out_shape=jax.ShapeDtypeStruct((rows, block), BF),
        compiler_params=pltpu.CompilerParams(vmem_limit_bytes=16 * 2**20),
        cost_estimate=pl.CostEstimate(
            flops=6 * rows * block * units,
            bytes_accessed=6 * rows * block + 6 * block * units,
            transcendentals=rows * units,
        ),
    )(normed, hidden, *weights)


def mlp_backward(weights, normed, cot):
    rows, block = normed.shape
    units = weights[0].shape[1]
    tile = min(512, rows)
    return pl.pallas_call(
        functools.partial(mlp_backward_kernel, min(256, units)),
        grid=(rows // tile,),
        in_specs=row_specs(tile, block, block) + whole_specs(*weights),
        out_specs=row_specs(tile, units, units, units, block),
        out_shape=[jax.ShapeDtypeStruct((rows, units), BF)] * 3
        + [jax.ShapeDtypeStruct((rows, block), F32)],
        compiler_params=pltpu.CompilerParams(vmem_limit_bytes=22 * 2**20),
        cost_estimate=pl.CostEstimate(
            flops=10 * rows * block * units,
            bytes_accessed=8 * rows * block + 6 * block * units + 6 * rows * units,
            transcendentals=rows * units,
        ),
    )(normed, cot, *weights)


def normalise(hidden, width):
    wide = hidden.astype(F32)
    inv_rms = lax.rsqrt(sum_over_y(jnp.sum(wide * wide, axis=-1)) / width + norm_eps)[..., None]
    return inv_rms, (wide * inv_rms).astype(BF)


def normalise_backward(hidden, inv_rms, upstream, grad_normed, width):
    wide = hidden.astype(F32)
    centred = sum_over_y(jnp.sum(grad_normed * wide, axis=-1))[..., None] / width
    return upstream.astype(F32) + inv_rms * grad_normed - wide * inv_rms**3 * centred


def mlp_weight_grads(normed, cot, active, grad_gate, grad_up):
    return (
        product("rf,rd->fd", grad_gate, normed).astype(BF),
        product("rf,rd->fd", grad_up, normed).astype(BF),
        product("rf,rd->fd", active, cot).astype(BF),
    )


def pack_kernel(ny, per, place_ref, *refs):
    time_refs, spectral_refs, out_ref = refs[:2], refs[2:4], refs[4]
    section, y, core = place_ref[0], place_ref[1], place_ref[2]
    size = time_refs[0].shape[1]
    q = lax.broadcasted_iota(jnp.int32, (size, size), 0)
    a = lax.broadcasted_iota(jnp.int32, (size, size), 1)
    back, sib = (q // per) % ny, q // (per * ny)
    natural = lax.rem(y + ny - back, ny) * (2 * per) + (core ^ sib) * per + q % per
    order = (natural == a).astype(BF)

    def load(pair, rows, start):
        picked = [ref[pl.ds(rows * per, per), pl.ds(pl.multiple_of(start, per), per), :] for ref in pair]
        value = jnp.where(section == 0, picked[0], picked[1])
        return value.reshape(per * per, size)

    for to in range(ny):
        rows = lax.rem(y + ny - to, ny)
        for rep in range(2 * ny):
            from_y, from_core = rep // 2, rep % 2
            group = (core ^ from_core) * ny + lax.rem(y + ny - from_y, ny)
            time = load(time_refs, rows, group * per)
            spectral = dot(load(spectral_refs, rows, rep * per).astype(BF), order)
            out_ref[to * 2 * ny + rep] = jnp.concatenate([time, spectral], axis=1).astype(BF)


def pack_factors(ny, per, place, time_grads, spectral_grads):
    size = time_grads[0].shape[1]
    return pl.pallas_call(
        functools.partial(pack_kernel, ny, per),
        in_specs=[pl.BlockSpec(memory_space=pltpu.SMEM)] + [pl.BlockSpec(memory_space=pltpu.VMEM)] * 4,
        out_shape=jax.ShapeDtypeStruct((ny * 2 * ny, per * per, 2 * size), BF),
        compiler_params=pltpu.CompilerParams(vmem_limit_bytes=12 * 2**20),
    )(place, *time_grads, *spectral_grads)


def totals_kernel(factor_ref, kernel_ref, mlp_ref, sum_ref, square_ref):
    factor = jnp.sum(factor_ref[...].astype(F32), axis=0)
    sum_ref[...] = factor
    half = factor.shape[1] // 2
    lanes = lax.broadcasted_iota(jnp.int32, factor.shape, 1)
    squared = factor * factor
    kernel = kernel_ref[...].astype(F32)
    terms = [
        jnp.where(lanes < half, squared, 0.0),
        jnp.where(lanes < half, 0.0, squared),
        jnp.sum(kernel * kernel, axis=0),
    ]
    for member in range(mlp_ref.shape[0]):
        value = jnp.sum(mlp_ref[member] * mlp_ref[member], axis=0)
        terms.append(value)
    places = lax.broadcasted_iota(jnp.int32, square_ref.shape[1:], 1)
    squares = jnp.zeros(square_ref.shape[1:], F32)
    for member, term in enumerate(terms):
        squares = jnp.where(places == member, jnp.sum(term, axis=(0, 1), keepdims=True), squares)
    square_ref[...] = jnp.broadcast_to(squares[None], square_ref.shape)


def totals(copies, factor, kernel, mlp):
    return pl.pallas_call(
        totals_kernel,
        out_shape=[
            jax.ShapeDtypeStruct(factor.shape[1:], F32),
            jax.ShapeDtypeStruct((copies, 1, 128), F32),
        ],
    )(factor, kernel, mlp)


def update_kernel(counts, square_ref, *refs):
    total = jnp.sum(square_ref[...], axis=0)
    members = len(counts)
    for member, count in enumerate(counts):
        inv_scale = lax.rsqrt(total[:, member : member + 1] / count + norm_eps)
        momentum, part, out = (refs[member + group * members] for group in range(3))
        value = part[...].astype(F32)
        scale = jnp.reshape(inv_scale, (1,) * value.ndim)
        out[...] = momentum_coef * momentum[...] + value * scale


def update(counts, squares, momenta, parts):
    return pl.pallas_call(
        functools.partial(update_kernel, counts),
        out_shape=[jax.ShapeDtypeStruct(momentum.shape, F32) for momentum in momenta],
    )(squares, *momenta, *parts)


def gather_over_y(sent, own):
    count = lax.axis_size("y")
    moved = [
        lax.ppermute(sent(step), "y", [(i, (i + step) % count) for i in range(count)])
        for step in range(1, count)
    ]
    return [own] + moved


def spread_rows(values):
    count, y = lax.axis_size("y"), lax.axis_index("y")
    block = values.shape[1] // count

    def piece(step):
        return lax.dynamic_slice_in_dim(values, ((y + step) % count) * block, block, 1)

    return gather_over_y(piece, piece(0))


def barrier(*values):
    return lax.optimization_barrier(values)


def shards(
    tokens_in,
    lengths,
    cotangent,
    time_blocks,
    spectral_blocks,
    spectral_kernel,
    gate_weight,
    up_weight,
    down_weight,
    momentum_time,
    momentum_spectral,
    momentum_kernel,
    momentum_gate,
    momentum_up,
    momentum_down,
):
    ny, nc, nr = lax.axis_size("y"), lax.axis_size("core"), lax.axis_size("rep")
    section, y, core = lax.axis_index("section"), lax.axis_index("y"), lax.axis_index("core")
    _, row_count, width = tokens_in.shape
    block = width // ny
    per = time_blocks.shape[1]
    size = time_blocks.shape[2]
    mine = per * ny
    first_layer = section == 0

    flat = (mine * size, block)
    cube = (mine, size, block)

    place = jnp.arange(size, dtype=jnp.int32)
    from_core = core ^ (place // (ny * per))
    from_y = (y - place // per) % ny
    natural = from_y * (nc * per) + from_core * per + place % per
    order = (natural[:, None] == place[None, :]).astype(BF)

    factors = jnp.concatenate([time_blocks[0], spectral_blocks[0]], axis=-1).reshape(-1, 2 * size)
    other_factors = section_swap(factors)
    own_kernel = spread_rows(spectral_kernel[0].reshape(per * size, width))

    own_mlp = [
        lax.dynamic_index_in_dim(weight[0], y, 0, keepdims=False)
        for weight in (gate_weight, up_weight, down_weight)
    ]
    hidden_units = down_weight.shape[2]
    half = hidden_units // 2
    sent = [
        lax.dynamic_slice_in_dim(weight, core * half, half, axis)
        for weight, axis in zip(own_mlp, (1, 1, 0))
    ]
    got = section_swap(jnp.concatenate(sent[:2] + [sent[2][:block], sent[2][block:]], axis=1))

    positions = (y * nc + core) * row_count + jnp.arange(row_count, dtype=jnp.int32)
    keep = (positions < lengths[0])[:, None]
    factors = jnp.concatenate(
        [
            jnp.where(first_layer, factors, other_factors),
            jnp.where(first_layer, other_factors, factors),
        ],
        axis=1,
    )
    own_kernel = jnp.concatenate(own_kernel).reshape(cube)
    own_kernel, factors, tokens, got = barrier(own_kernel, factors, tokens_in[0], got)
    other_kernel = section_swap(own_kernel)
    tokens = jnp.where(keep, tokens, jnp.zeros_like(tokens))

    def tokens_and_factors(step):
        piece = lax.dynamic_slice_in_dim(tokens, ((y + step) % ny) * block, block, 1)
        return jnp.concatenate([piece, factors])

    joined = gather_over_y(tokens_and_factors, tokens_and_factors(0))
    sibling = core_swap(got)
    other_mlp = [
        jnp.concatenate([got[:, :half], sibling[:, :half]], axis=1),
        jnp.concatenate([got[:, half : 2 * half], sibling[:, half : 2 * half]], axis=1),
        jnp.concatenate(
            [
                packed[:, 2 * half + start : 2 * half + start + block]
                for packed in (got, sibling)
                for start in (0, block)
            ]
        ),
    ]
    mlp_all = [
        [jnp.where(first_layer, one, two) for one, two in zip(own_mlp, other_mlp)],
        [jnp.where(first_layer, two, one) for one, two in zip(own_mlp, other_mlp)],
    ]
    inputs = jnp.concatenate([piece[:row_count] for piece in joined]).reshape(cube)
    factors = jnp.concatenate([piece[row_count:] for piece in joined]).reshape(mine, size, -1)
    time_all = [
        product("qi,aij->aqj", order, factors[..., start : start + size]).astype(BF)
        for start in (0, 2 * size)
    ]
    spectral_all = [
        product("bia,qa->biq", factors[..., start : start + size], order).astype(BF)
        for start in (size, 3 * size)
    ]
    weights = mlp_all[0] + mlp_all[1]
    inputs, *weights = barrier(inputs, *weights)
    mlp_all = [weights[:3], weights[3:]]
    kernel_all = [
        jnp.where(first_layer, own_kernel, other_kernel),
        jnp.where(first_layer, other_kernel, own_kernel),
    ]

    activations = inputs
    stash = []
    for layer in range(2):
        hidden, mix_saved = mixer_forward(
            time_all[layer], spectral_all[layer], kernel_all[layer], activations
        )
        hidden = hidden.reshape(flat)
        inv_rms, normed = normalise(hidden, width)
        stash.append((hidden, mix_saved, inv_rms, normed))
        if layer == 0:
            seed, normed = barrier(cotangent[0], normed)
            upstream = spread_rows(jnp.where(keep, seed, jnp.zeros_like(seed)))
            activations = mlp_forward(mlp_all[layer], normed, hidden).reshape(cube)
            activations, *upstream = barrier(activations, *upstream)
            upstream = jnp.concatenate(upstream)
    def reduce_mlp(layer_grads):
        picked = [jnp.where(first_layer, one, two) for one, two in zip(*layer_grads)]
        picked = jnp.stack(picked).reshape(3, ny, nc, nr, -1, block)
        keep_half = lax.dynamic_index_in_dim(picked, core, 2, keepdims=False)
        send_half = lax.dynamic_index_in_dim(picked, 1 - core, 2, keepdims=False)
        halves = (keep_half.astype(F32) + core_swap(send_half).astype(F32)).astype(BF)
        return jnp.transpose(halves, (1, 2, 0, 3, 4)).reshape(ny * nr, 3, -1, block)

    time_grads, spectral_grads, kernel_grads, mlp_grads = ([None, None] for _ in range(4))
    for layer in (1, 0):
        hidden, mix_saved, inv_rms, normed = stash[layer]
        cot = upstream.reshape(flat)
        active, grad_gate, grad_up, grad_normed = mlp_backward(mlp_all[layer], normed, cot)
        grad_hidden = normalise_backward(hidden, inv_rms, cot, grad_normed, width)
        mlp_grads[layer] = mlp_weight_grads(normed, cot, active, grad_gate, grad_up)
        grad_hidden, *mlp_grads[layer] = barrier(grad_hidden, *mlp_grads[layer])
        mlp_grad = reduce_mlp(mlp_grads) if layer == 0 else None
        upstream, mix_grads, mlp_grad = mixer_backward(
            time_all[layer],
            spectral_all[layer],
            kernel_all[layer],
            mix_saved,
            grad_hidden.reshape(cube),
            mlp_grad,
        )
        time_grads[layer], spectral_grads[layer], kernel_grads[layer] = mix_grads

    kernel_grad = jnp.where(first_layer, *kernel_grads)
    mlp_grad = jnp.sum(mlp_grad.reshape(ny, nr, 3, -1, block).astype(F32), axis=1)
    mlp_grad = jnp.transpose(mlp_grad, (1, 0, 2, 3)).reshape(3, -1, block)

    place = jnp.stack([section, y, core]).astype(jnp.int32)
    factor_grad = pack_factors(ny, per, place, time_grads, spectral_grads)

    rep = lax.axis_index("rep")
    near = nr // 2
    z = rep % near
    kernel_grad = kernel_grad.reshape(2, ny // 2, per * size, block)

    def kernel_pieces(to):
        start = (0, to // 2, 0, (to % 2) * (block // 2))
        return lax.dynamic_slice(kernel_grad, start, (2, 1, per * size, block // 2))[:, 0]

    moved = [
        lax.ppermute(kernel_pieces(z ^ flip), "rep", [(i, i ^ flip) for i in range(nr)])
        for flip in range(1, near)
    ]
    *moved, _ = barrier(*moved, factor_grad)
    kernel_sum = kernel_pieces(z).astype(F32)
    for piece in moved:
        kernel_sum = kernel_sum + piece.astype(F32)
    kernel_sum = kernel_sum.astype(BF)
    x = rep // near
    part_kernel = 0.0
    for turn in range(2):
        holders = [
            (k * nr + ((2 * back + side) ^ (near * turn)), ((k - back) % ny) * nr + 2 * k + side)
            for k in range(ny)
            for back in range(ny)
            for side in range(2)
        ]
        piece = lax.dynamic_index_in_dim(kernel_sum, x ^ turn, 0, keepdims=False)
        part_kernel = part_kernel + lax.ppermute(piece, ("y", "rep"), holders).astype(F32)
    part_kernel = part_kernel.reshape(per, size, block // 2)
    factor_grad = lax.all_to_all(factor_grad, ("y", "rep"), 0, 0, tiled=True)

    everyone = ny * nc * nr
    factor_sum, squares = totals(
        everyone, factor_grad, part_kernel.reshape(-1, size, 2 * size), mlp_grad.reshape(3, -1, 8, 128)
    )
    squares = lax.all_to_all(squares, ("y", "core", "rep"), 0, 0, tiled=True)
    parts = (
        factor_sum[:, :size],
        factor_sum[:, size:],
        part_kernel,
        *(mlp_grad[member].reshape(ny, -1, block) for member in range(3)),
    )
    counts = (
        time_blocks[0].size * ny * nc,
        spectral_blocks[0].size * ny * nc,
        spectral_kernel[0].size * ny * nc,
        gate_weight[0].size,
        up_weight[0].size,
        down_weight[0].size,
    )
    momenta = (
        momentum_time.reshape(size, size),
        momentum_spectral.reshape(size, size),
        momentum_kernel[0],
        jnp.swapaxes(momentum_gate[0], 1, 2),
        jnp.swapaxes(momentum_up[0], 1, 2),
        momentum_down[0],
    )
    new = update(counts, squares, momenta, parts)
    return (
        new[0].reshape(momentum_time.shape),
        new[1].reshape(momentum_spectral.shape),
        new[2][None],
        jnp.swapaxes(new[3], 1, 2)[None],
        jnp.swapaxes(new[4], 1, 2)[None],
        new[5][None],
    )


def solution(mesh):
    sections, seqs, reps = (mesh.shape[name] for name in ("section", "seq", "rep"))
    split = Mesh(
        mesh.devices.reshape(sections, seqs // 2, 2, reps), ("section", "y", "core", "rep")
    )
    seq = ("y", "core")
    everyone = ("y", "core", "rep")
    placed = (
        P("rep", seq, None),
        P("rep"),
        P("rep", seq, None),
        P("section", seq, None, None),
        P("section", seq, None, None),
        P("section", seq, None, None),
        P("section", None, None, None),
        P("section", None, None, None),
        P("section", None, None, None),
        P("section", seq, "rep", None),
        P("section", seq, "rep", None),
        P("section", seq, None, "rep"),
        P("section", None, None, everyone),
        P("section", None, None, everyone),
        P("section", None, everyone, None),
    )
    return jax.shard_map(
        shards,
        mesh=split,
        in_specs=placed,
        out_specs=placed[9:],
        check_vma=False,
    )
```

```python
import functools

import jax
import jax.numpy as jnp
from jax import lax
from jax.experimental import pallas as pl
from jax.experimental.pallas import tpu as pltpu
from jax.sharding import Mesh
from jax.sharding import PartitionSpec as P

momentum_coef = 0.9
norm_eps = 1e-06
BF = jnp.bfloat16
F32 = jnp.float32


def product(pattern, first_operand, second_operand):
    return jnp.einsum(pattern, first_operand, second_operand, preferred_element_type=F32)


def core_swap(value):
    return lax.ppermute(value, "core", [(0, 1), (1, 0)])


def section_swap(value):
    return lax.ppermute(value, "section", [(0, 1), (1, 0)])


def sum_over_y(value):
    count = lax.axis_size("y")
    total = value
    for step in range(1, count):
        moved = lax.ppermute(value, "y", [(i, (i + step) % count) for i in range(count)])
        total = total + jnp.roll(moved, step * (value.shape[0] // count))
    return total


def time_mix_forward(time_mix, values):
    mixed = product("aij,ajc->iac", time_mix, values).astype(BF)
    half = mixed.shape[0] // 2
    return mixed[:half], mixed[half:]


def to_columns(time_mix, values):
    own, other = time_mix_forward(time_mix, values)
    return jnp.concatenate([own, core_swap(other)], axis=1)


def to_rows(blocks):
    half = blocks.shape[1] // 2
    own, other = blocks[:, :half], blocks[:, half:]
    return jnp.concatenate([own, core_swap(other)], axis=0)


def mixer_forward(time_mix, spectral_mix, kernel, inputs):
    columns = to_columns(time_mix, inputs)
    spectrum = product("bij,bjc->bic", spectral_mix, columns)
    weighted = (kernel.astype(F32) * spectrum).astype(BF)
    returned = product("bji,bjc->bic", spectral_mix, weighted).astype(BF)
    rows_back = to_rows(returned)
    mixed = product("aji,jac->aic", time_mix, rows_back)
    hidden = (inputs.astype(F32) + mixed).astype(BF)
    return hidden, (inputs, columns, spectrum.astype(BF), weighted, rows_back)


def mixer_backward(time_mix, spectral_mix, kernel, stored, grad_hidden, sent):
    inputs, columns, spectrum, weighted, rows_back = stored
    grad_mixed = grad_hidden.astype(BF)
    grad_cols = to_columns(time_mix, grad_mixed)
    if sent is not None:
        sent, grad_cols = barrier(sent, grad_cols)
        sent = lax.all_to_all(sent, ("y", "rep"), 0, 0, tiled=True)
    time_grad = product("iac,ajc->aij", rows_back, grad_mixed)
    grad_weighted = product("bji,bic->bjc", spectral_mix, grad_cols)
    spectral_grad = product("bjc,bic->bji", weighted, grad_cols)
    kernel_grad = (grad_weighted * spectrum.astype(F32)).astype(BF)
    grad_spectrum = (grad_weighted * kernel.astype(F32)).astype(BF)
    grad_columns = product("bij,bic->bjc", spectral_mix, grad_spectrum).astype(BF)
    spectral_grad = spectral_grad + product("bic,bjc->bij", grad_spectrum, columns)
    grad_rows = to_rows(grad_columns)
    if sent is not None:
        sent, grad_rows = barrier(sent, grad_rows)
    time_grad = time_grad + product("iac,ajc->aij", grad_rows, inputs)
    entry = None
    if sent is None:
        entry = (grad_hidden + product("aij,iac->ajc", time_mix, grad_rows)).astype(BF)
    return entry, (time_grad, spectral_grad, kernel_grad), sent


def dot(first_operand, second_operand, dims=((1,), (0,))):
    return lax.dot_general(first_operand, second_operand, (dims, ((), ())), preferred_element_type=F32)


def sigmoid(value):
    return 0.5 * jnp.tanh(0.5 * value) + 0.5


def mlp_forward_kernel(chunk, normed_ref, hidden_ref, gate_ref, up_ref, down_ref, out_ref):
    normed = normed_ref[...]
    total = hidden_ref[...].astype(F32)
    for start in range(0, gate_ref.shape[1], chunk):
        part = slice(start, start + chunk)
        gate = dot(normed, gate_ref[:, part])
        upper = dot(normed, up_ref[:, part])
        active = (gate * sigmoid(gate) * upper).astype(BF)
        total = total + dot(active, down_ref[part, :])
    out_ref[...] = total.astype(BF)


def mlp_backward_kernel(
    chunk, normed_ref, cot_ref, gate_ref, up_ref, down_ref, active_ref, grad_gate_ref, grad_up_ref, out_ref
):
    normed, cot = normed_ref[...], cot_ref[...]
    total = None
    for start in range(0, gate_ref.shape[1], chunk):
        part = slice(start, start + chunk)
        gate = dot(normed, gate_ref[:, part])
        upper = dot(normed, up_ref[:, part])
        grad_active = dot(cot, down_ref[part, :], ((1,), (1,)))
        sigma = sigmoid(gate)
        silu = gate * sigma
        active_ref[:, part] = (silu * upper).astype(BF)
        grad_up = (grad_active * silu).astype(BF)
        grad_gate = (grad_active * upper * (sigma + silu * (1.0 - sigma))).astype(BF)
        grad_up_ref[:, part] = grad_up
        grad_gate_ref[:, part] = grad_gate
        both_grads = jnp.concatenate([grad_gate, grad_up], axis=1)
        both_weights = jnp.concatenate([gate_ref[:, part], up_ref[:, part]], axis=1)
        term = dot(both_grads, both_weights, ((1,), (1,)))
        total = term if total is None else total + term
    out_ref[...] = total


def row_specs(tile, *widths):
    return [pl.BlockSpec((tile, width), lambda i: (i, 0)) for width in widths]


def whole_specs(*arrays):
    return [pl.BlockSpec(array.shape, lambda i, n=array.ndim: (0,) * n) for array in arrays]


def mlp_forward(weights, normed, hidden):
    rows, block = normed.shape
    units = weights[0].shape[1]
    tile = min(512, rows)
    return pl.pallas_call(
        functools.partial(mlp_forward_kernel, min(256, units)),
        grid=(rows // tile,),
        in_specs=row_specs(tile, block, block) + whole_specs(*weights),
        out_specs=row_specs(tile, block)[0],
        out_shape=jax.ShapeDtypeStruct((rows, block), BF),
        compiler_params=pltpu.CompilerParams(vmem_limit_bytes=16 * 2**20),
        cost_estimate=pl.CostEstimate(
            flops=6 * rows * block * units,
            bytes_accessed=6 * rows * block + 6 * block * units,
            transcendentals=rows * units,
        ),
    )(normed, hidden, *weights)


def mlp_backward(weights, normed, cot):
    rows, block = normed.shape
    units = weights[0].shape[1]
    tile = min(512, rows)
    return pl.pallas_call(
        functools.partial(mlp_backward_kernel, min(256, units)),
        grid=(rows // tile,),
        in_specs=row_specs(tile, block, block) + whole_specs(*weights),
        out_specs=row_specs(tile, units, units, units, block),
        out_shape=[jax.ShapeDtypeStruct((rows, units), BF)] * 3
        + [jax.ShapeDtypeStruct((rows, block), F32)],
        compiler_params=pltpu.CompilerParams(vmem_limit_bytes=22 * 2**20),
        cost_estimate=pl.CostEstimate(
            flops=10 * rows * block * units,
            bytes_accessed=8 * rows * block + 6 * block * units + 6 * rows * units,
            transcendentals=rows * units,
        ),
    )(normed, cot, *weights)


def normalise(hidden, width):
    wide = hidden.astype(F32)
    inv_rms = lax.rsqrt(sum_over_y(jnp.sum(wide * wide, axis=-1)) / width + norm_eps)[..., None]
    return inv_rms, (wide * inv_rms).astype(BF)


def normalise_backward(hidden, inv_rms, upstream, grad_normed, width):
    wide = hidden.astype(F32)
    centred = sum_over_y(jnp.sum(grad_normed * wide, axis=-1))[..., None] / width
    return upstream.astype(F32) + inv_rms * grad_normed - wide * inv_rms**3 * centred


def mlp_weight_grads(normed, cot, active, grad_gate, grad_up):
    return (
        product("rf,rd->fd", grad_gate, normed).astype(BF),
        product("rf,rd->fd", grad_up, normed).astype(BF),
        product("rf,rd->fd", active, cot).astype(BF),
    )


def pack_kernel(ny, per, place_ref, *refs):
    time_refs, spectral_refs, out_ref = refs[:2], refs[2:4], refs[4]
    section, y, core = place_ref[0], place_ref[1], place_ref[2]
    size = time_refs[0].shape[1]
    q = lax.broadcasted_iota(jnp.int32, (size, size), 0)
    a = lax.broadcasted_iota(jnp.int32, (size, size), 1)
    back, sib = (q // per) % ny, q // (per * ny)
    natural = lax.rem(y + ny - back, ny) * (2 * per) + (core ^ sib) * per + q % per
    order = (natural == a).astype(BF)

    def load(pair, rows, start):
        picked = [ref[pl.ds(rows * per, per), pl.ds(pl.multiple_of(start, per), per), :] for ref in pair]
        value = jnp.where(section == 0, picked[0], picked[1])
        return value.reshape(per * per, size)

    for to in range(ny):
        rows = lax.rem(y + ny - to, ny)
        for rep in range(2 * ny):
            from_y, from_core = rep // 2, rep % 2
            group = (core ^ from_core) * ny + lax.rem(y + ny - from_y, ny)
            time = load(time_refs, rows, group * per)
            spectral = dot(load(spectral_refs, rows, rep * per).astype(BF), order)
            out_ref[to * 2 * ny + rep] = jnp.concatenate([time, spectral], axis=1).astype(BF)


def pack_factors(ny, per, place, time_grads, spectral_grads):
    size = time_grads[0].shape[1]
    return pl.pallas_call(
        functools.partial(pack_kernel, ny, per),
        in_specs=[pl.BlockSpec(memory_space=pltpu.SMEM)] + [pl.BlockSpec(memory_space=pltpu.VMEM)] * 4,
        out_shape=jax.ShapeDtypeStruct((ny * 2 * ny, per * per, 2 * size), BF),
        compiler_params=pltpu.CompilerParams(vmem_limit_bytes=12 * 2**20),
    )(place, *time_grads, *spectral_grads)


def totals_kernel(factor_ref, kernel_ref, mlp_ref, sum_ref, square_ref):
    factor = jnp.sum(factor_ref[...].astype(F32), axis=0)
    sum_ref[...] = factor
    half = factor.shape[1] // 2
    lanes = lax.broadcasted_iota(jnp.int32, factor.shape, 1)
    squared = factor * factor
    kernel = kernel_ref[...].astype(F32)
    terms = [
        jnp.where(lanes < half, squared, 0.0),
        jnp.where(lanes < half, 0.0, squared),
        jnp.sum(kernel * kernel, axis=0),
    ]
    for member in range(mlp_ref.shape[0]):
        value = jnp.sum(mlp_ref[member] * mlp_ref[member], axis=0)
        terms.append(value)
    places = lax.broadcasted_iota(jnp.int32, square_ref.shape[1:], 1)
    squares = jnp.zeros(square_ref.shape[1:], F32)
    for member, term in enumerate(terms):
        squares = jnp.where(places == member, jnp.sum(term, axis=(0, 1), keepdims=True), squares)
    square_ref[...] = jnp.broadcast_to(squares[None], square_ref.shape)


def totals(copies, factor, kernel, mlp):
    return pl.pallas_call(
        totals_kernel,
        out_shape=[
            jax.ShapeDtypeStruct(factor.shape[1:], F32),
            jax.ShapeDtypeStruct((copies, 1, 128), F32),
        ],
    )(factor, kernel, mlp)


def update_kernel(counts, square_ref, *refs):
    total = jnp.sum(square_ref[...], axis=0)
    members = len(counts)
    for member, count in enumerate(counts):
        inv_scale = lax.rsqrt(total[:, member : member + 1] / count + norm_eps)
        momentum, part, out = (refs[member + group * members] for group in range(3))
        value = part[...].astype(F32)
        scale = jnp.reshape(inv_scale, (1,) * value.ndim)
        out[...] = momentum_coef * momentum[...] + value * scale


def update(counts, squares, momenta, parts):
    return pl.pallas_call(
        functools.partial(update_kernel, counts),
        out_shape=[jax.ShapeDtypeStruct(momentum.shape, F32) for momentum in momenta],
    )(squares, *momenta, *parts)


def gather_over_y(sent, own):
    count = lax.axis_size("y")
    moved = [
        lax.ppermute(sent(step), "y", [(i, (i + step) % count) for i in range(count)])
        for step in range(1, count)
    ]
    return [own] + moved


def spread_rows(values):
    count, y = lax.axis_size("y"), lax.axis_index("y")
    block = values.shape[1] // count

    def piece(step):
        return lax.dynamic_slice_in_dim(values, ((y + step) % count) * block, block, 1)

    return gather_over_y(piece, piece(0))


def barrier(*values):
    return lax.optimization_barrier(values)


def shards(
    tokens_in,
    lengths,
    cotangent,
    time_blocks,
    spectral_blocks,
    spectral_kernel,
    gate_weight,
    up_weight,
    down_weight,
    momentum_time,
    momentum_spectral,
    momentum_kernel,
    momentum_gate,
    momentum_up,
    momentum_down,
):
    ny, nc, nr = lax.axis_size("y"), lax.axis_size("core"), lax.axis_size("rep")
    section, y, core = lax.axis_index("section"), lax.axis_index("y"), lax.axis_index("core")
    _, row_count, width = tokens_in.shape
    block = width // ny
    per = time_blocks.shape[1]
    size = time_blocks.shape[2]
    mine = per * ny
    first_layer = section == 0

    flat = (mine * size, block)
    cube = (mine, size, block)

    place = jnp.arange(size, dtype=jnp.int32)
    from_core = core ^ (place // (ny * per))
    from_y = (y - place // per) % ny
    natural = from_y * (nc * per) + from_core * per + place % per
    order = (natural[:, None] == place[None, :]).astype(BF)

    factors = jnp.concatenate([time_blocks[0], spectral_blocks[0]], axis=-1).reshape(-1, 2 * size)
    other_factors = section_swap(factors)
    own_kernel = spread_rows(spectral_kernel[0].reshape(per * size, width))

    own_mlp = [
        lax.dynamic_index_in_dim(weight[0], y, 0, keepdims=False)
        for weight in (gate_weight, up_weight, down_weight)
    ]
    hidden_units = down_weight.shape[2]
    half = hidden_units // 2
    sent = [
        lax.dynamic_slice_in_dim(weight, core * half, half, axis)
        for weight, axis in zip(own_mlp, (1, 1, 0))
    ]
    got = section_swap(jnp.concatenate(sent[:2] + [sent[2][:block], sent[2][block:]], axis=1))

    positions = (y * nc + core) * row_count + jnp.arange(row_count, dtype=jnp.int32)
    keep = (positions < lengths[0])[:, None]
    factors = jnp.concatenate(
        [
            jnp.where(first_layer, factors, other_factors),
            jnp.where(first_layer, other_factors, factors),
        ],
        axis=1,
    )
    own_kernel = jnp.concatenate(own_kernel).reshape(cube)
    own_kernel, factors, tokens, got = barrier(own_kernel, factors, tokens_in[0], got)
    other_kernel = section_swap(own_kernel)
    tokens = jnp.where(keep, tokens, jnp.zeros_like(tokens))

    def tokens_and_factors(step):
        piece = lax.dynamic_slice_in_dim(tokens, ((y + step) % ny) * block, block, 1)
        return jnp.concatenate([piece, factors])

    joined = gather_over_y(tokens_and_factors, tokens_and_factors(0))
    sibling = core_swap(got)
    other_mlp = [
        jnp.concatenate([got[:, :half], sibling[:, :half]], axis=1),
        jnp.concatenate([got[:, half : 2 * half], sibling[:, half : 2 * half]], axis=1),
        jnp.concatenate(
            [
                packed[:, 2 * half + start : 2 * half + start + block]
                for packed in (got, sibling)
                for start in (0, block)
            ]
        ),
    ]
    mlp_all = [
        [jnp.where(first_layer, one, two) for one, two in zip(own_mlp, other_mlp)],
        [jnp.where(first_layer, two, one) for one, two in zip(own_mlp, other_mlp)],
    ]
    inputs = jnp.concatenate([piece[:row_count] for piece in joined]).reshape(cube)
    factors = jnp.concatenate([piece[row_count:] for piece in joined]).reshape(mine, size, -1)
    time_all = [
        product("qi,aij->aqj", order, factors[..., start : start + size]).astype(BF)
        for start in (0, 2 * size)
    ]
    spectral_all = [
        product("bia,qa->biq", factors[..., start : start + size], order).astype(BF)
        for start in (size, 3 * size)
    ]
    weights = mlp_all[0] + mlp_all[1]
    inputs, *weights = barrier(inputs, *weights)
    mlp_all = [weights[:3], weights[3:]]
    kernel_all = [
        jnp.where(first_layer, own_kernel, other_kernel),
        jnp.where(first_layer, other_kernel, own_kernel),
    ]

    activations = inputs
    stash = []
    for layer in range(2):
        hidden, mix_saved = mixer_forward(
            time_all[layer], spectral_all[layer], kernel_all[layer], activations
        )
        hidden = hidden.reshape(flat)
        inv_rms, normed = normalise(hidden, width)
        stash.append((hidden, mix_saved, inv_rms, normed))
        if layer == 0:
            seed, normed = barrier(cotangent[0], normed)
            upstream = spread_rows(jnp.where(keep, seed, jnp.zeros_like(seed)))
            activations = mlp_forward(mlp_all[layer], normed, hidden).reshape(cube)
            activations, *upstream = barrier(activations, *upstream)
            upstream = jnp.concatenate(upstream)
    def reduce_mlp(layer_grads):
        picked = [jnp.where(first_layer, one, two) for one, two in zip(*layer_grads)]
        picked = jnp.stack(picked).reshape(3, ny, nc, nr, -1, block)
        keep_half = lax.dynamic_index_in_dim(picked, core, 2, keepdims=False)
        send_half = lax.dynamic_index_in_dim(picked, 1 - core, 2, keepdims=False)
        halves = (keep_half.astype(F32) + core_swap(send_half).astype(F32)).astype(BF)
        return jnp.transpose(halves, (1, 2, 0, 3, 4)).reshape(ny * nr, 3, -1, block)

    time_grads, spectral_grads, kernel_grads, mlp_grads = ([None, None] for _ in range(4))
    for layer in (1, 0):
        hidden, mix_saved, inv_rms, normed = stash[layer]
        cot = upstream.reshape(flat)
        active, grad_gate, grad_up, grad_normed = mlp_backward(mlp_all[layer], normed, cot)
        grad_hidden = normalise_backward(hidden, inv_rms, cot, grad_normed, width)
        mlp_grads[layer] = mlp_weight_grads(normed, cot, active, grad_gate, grad_up)
        grad_hidden, *mlp_grads[layer] = barrier(grad_hidden, *mlp_grads[layer])
        mlp_grad = reduce_mlp(mlp_grads) if layer == 0 else None
        upstream, mix_grads, mlp_grad = mixer_backward(
            time_all[layer],
            spectral_all[layer],
            kernel_all[layer],
            mix_saved,
            grad_hidden.reshape(cube),
            mlp_grad,
        )
        time_grads[layer], spectral_grads[layer], kernel_grads[layer] = mix_grads

    kernel_grad = jnp.where(first_layer, *kernel_grads)
    mlp_grad = jnp.sum(mlp_grad.reshape(ny, nr, 3, -1, block).astype(F32), axis=1)
    mlp_grad = jnp.transpose(mlp_grad, (1, 0, 2, 3)).reshape(3, -1, block)

    place = jnp.stack([section, y, core]).astype(jnp.int32)
    factor_grad = pack_factors(ny, per, place, time_grads, spectral_grads)

    rep = lax.axis_index("rep")
    near = nr // 2
    z = rep % near
    kernel_grad = kernel_grad.reshape(2, ny // 2, per * size, block)

    def kernel_pieces(to):
        start = (0, to // 2, 0, (to % 2) * (block // 2))
        return lax.dynamic_slice(kernel_grad, start, (2, 1, per * size, block // 2))[:, 0]

    moved = [
        lax.ppermute(kernel_pieces(z ^ flip), "rep", [(i, i ^ flip) for i in range(nr)])
        for flip in range(1, near)
    ]
    *moved, _ = barrier(*moved, factor_grad)
    kernel_sum = kernel_pieces(z).astype(F32)
    for piece in moved:
        kernel_sum = kernel_sum + piece.astype(F32)
    kernel_sum = kernel_sum.astype(BF)
    x = rep // near
    part_kernel = 0.0
    for turn in range(2):
        holders = [
            (k * nr + ((2 * back + side) ^ (near * turn)), ((k - back) % ny) * nr + 2 * k + side)
            for k in range(ny)
            for back in range(ny)
            for side in range(2)
        ]
        piece = lax.dynamic_index_in_dim(kernel_sum, x ^ turn, 0, keepdims=False)
        part_kernel = part_kernel + lax.ppermute(piece, ("y", "rep"), holders).astype(F32)
    part_kernel = part_kernel.reshape(per, size, block // 2)
    factor_grad = lax.all_to_all(factor_grad, ("y", "rep"), 0, 0, tiled=True)

    everyone = ny * nc * nr
    factor_sum, squares = totals(
        everyone, factor_grad, part_kernel.reshape(-1, size, 2 * size), mlp_grad.reshape(3, -1, 8, 128)
    )
    squares = lax.all_to_all(squares, ("y", "core", "rep"), 0, 0, tiled=True)
    parts = (
        factor_sum[:, :size],
        factor_sum[:, size:],
        part_kernel,
        *(mlp_grad[member].reshape(ny, -1, block) for member in range(3)),
    )
    counts = (
        time_blocks[0].size * ny * nc,
        spectral_blocks[0].size * ny * nc,
        spectral_kernel[0].size * ny * nc,
        gate_weight[0].size,
        up_weight[0].size,
        down_weight[0].size,
    )
    momenta = (
        momentum_time.reshape(size, size),
        momentum_spectral.reshape(size, size),
        momentum_kernel[0],
        jnp.swapaxes(momentum_gate[0], 1, 2),
        jnp.swapaxes(momentum_up[0], 1, 2),
        momentum_down[0],
    )
    new = update(counts, squares, momenta, parts)
    return (
        new[0].reshape(momentum_time.shape),
        new[1].reshape(momentum_spectral.shape),
        new[2][None],
        jnp.swapaxes(new[3], 1, 2)[None],
        jnp.swapaxes(new[4], 1, 2)[None],
        new[5][None],
    )


def solution(mesh):
    sections, seqs, reps = (mesh.shape[name] for name in ("section", "seq", "rep"))
    split = Mesh(
        mesh.devices.reshape(sections, seqs // 2, 2, reps), ("section", "y", "core", "rep")
    )
    seq = ("y", "core")
    everyone = ("y", "core", "rep")
    placed = (
        P("rep", seq, None),
        P("rep"),
        P("rep", seq, None),
        P("section", seq, None, None),
        P("section", seq, None, None),
        P("section", seq, None, None),
        P("section", None, None, None),
        P("section", None, None, None),
        P("section", None, None, None),
        P("section", seq, "rep", None),
        P("section", seq, "rep", None),
        P("section", seq, None, "rep"),
        P("section", None, None, everyone),
        P("section", None, None, everyone),
        P("section", None, everyone, None),
    )
    return jax.shard_map(
        shards,
        mesh=split,
        in_specs=placed,
        out_specs=placed[9:],
        check_vma=False,
    )
```
